128 devices in a mesh: row: 8 (over x_lo, z), col: 16 (over x_hi, y, core).
Axes of the slice: x: 4 (x_hi: 2, x_lo: 2; x = x_hi * 2 + x_lo), y: 4, z: 4, core: 2. Of those that a mesh axis runs over, the one named last changes fastest.
Arguments:
- points: float32 [16, 32768], P(None, ('row', 'col')), may hold values from -6 to 6
- inverse_scales: float32 [16], replicated, may hold values from 0.05 to 31.255105
- probe_signs: int32 [32768, 128], P(('row', 'col')), may hold values 0 or 1
Outputs:
- trace_terms: float32 [128], replicated
- logdet_terms: float32 [128], replicated
The draws below stay inside these ranges and needn't reach their ends.
All inputs are finite; a program needn't handle non-finite values. No bound on the sum of `probe_signs` on one device may be relied on, other than what follows from the above.
Results may differ from the reference program's by a relative error of at most 0.0014.
Values may be sent and summed in bfloat16 or wider, within the bound.
No kernel may reach another device: no remote copies, remote signals or barrier semaphores. Data moves between devices by JAX's collectives and lax.ppermute only.
A program may use at most 64 MiB of HBM per device.

```python
import math
import jax
import jax.numpy as jnp
from jax import lax

N = 32768
DIM = 16
PROBES = 128
STEPS = 3


def cluster_table(key):
    level_key, slot_key = jax.random.split(jax.random.fold_in(key, 29))
    positions = jnp.arange(N, dtype=jnp.int32)
    level_draw = jax.random.randint(level_key, (N,), 0, 6)
    levels = jnp.minimum(level_draw, 3)
    block_sizes = [max(N // 128, 1), max(N // 32, 1), max(N // 8, 1), N]
    counts = [max(block_sizes[0] // 60, 1), max(block_sizes[1] // 60, 1), max(block_sizes[2] // 60, 1), max(N // 20, 1)]
    raw_slots = jax.random.randint(slot_key, (N,), 0, 1 << 20)
    table_rows = jnp.zeros((N,), jnp.int32)
    for level_num in range(4):
        slot_ids = raw_slots % counts[level_num]
        candidate = level_num * N + positions // block_sizes[level_num] * counts[level_num] + slot_ids
        table_rows = jnp.where(levels == level_num, candidate, table_rows)
    return table_rows.astype(jnp.int32)


def draw_points(key, part):
    table_rows = cluster_table(key)
    centre_key, jitter_key = jax.random.split(jax.random.fold_in(key, 41))
    centres = jax.random.normal(centre_key, (DIM, 4 * N), jnp.float32)
    jitter = 0.5 * jax.random.normal(jitter_key, (DIM, N), jnp.float32)
    return jnp.clip(centres[:, table_rows] + jitter, -6.0, 6.0)


def draw_inverse_scales(key, part):
    second_key = jax.random.fold_in(jax.random.fold_in(key, 17), 1)
    return jnp.exp(jax.random.uniform(second_key, (DIM,), jnp.float32, math.log(0.25), math.log(0.5)))


def touch_ends(array, stream_key, low, largest):
    longest = array.shape.index(max(array.shape))
    spots = []
    for shift in (0, 1):
        where = [jax.random.randint(jax.random.fold_in(stream_key, axis), (), 0, length) for axis, length in enumerate(array.shape)]
        where[longest] = (where[longest] + shift) % array.shape[longest]
        spots.append(tuple(where))
    return array.at[spots[0]].set(low).at[spots[1]].set(largest)


def setup_inputs(seed: int = 0) -> dict:
    key_of = jax.random.split(jax.random.key(seed), 4)
    points = draw_points(jax.random.fold_in(key_of[3], 71), 0)
    inverse_scales = draw_inverse_scales(jax.random.fold_in(key_of[3], 71), 0)
    probe_signs = touch_ends((jax.random.randint(key_of[2], (N, PROBES), 0, 2) < 1).astype(jnp.int32), jax.random.fold_in(key_of[2], 1), 0, 1)
    return {"points": points, "inverse_scales": inverse_scales, "probe_signs": probe_signs}


epsilon = 1e-06
noise_level = 1.0
jacobi_sweeps = 6

def kernel_block(left_points, right_points):
    cross_term = lax.dot_general(left_points, right_points, (((0,), (0,)), ((), ())), precision=lax.Precision.HIGHEST, preferred_element_type=jnp.float32)
    left_norms = lax.optimization_barrier(jnp.sum(left_points * left_points, axis=0))
    right_norms = lax.optimization_barrier(jnp.sum(right_points * right_points, axis=0))
    distance = jnp.maximum(left_norms[:, None] + right_norms[None, :] - 2.0 * cross_term, 0.0)
    return jnp.exp(-0.5 * distance).astype(jnp.bfloat16)

def apply_kernel(scaled, vector_half):
    total_rows = scaled.shape[1]
    block_rows = math.gcd(total_rows, 2048)
    blocked = scaled.reshape(scaled.shape[0], total_rows // block_rows, block_rows).transpose(1, 0, 2)
    products = lax.map(lambda block_points: jnp.dot(kernel_block(block_points, scaled), vector_half, preferred_element_type=jnp.float32), blocked)
    return products.reshape(total_rows, vector_half.shape[1])

def log_weight(alpha_list, beta_list):
    degree = len(alpha_list)
    width_probes = alpha_list[0].shape[0]
    zeros_row = jnp.zeros((width_probes,), jnp.float32)
    ones_row = jnp.ones((width_probes,), jnp.float32)
    matrix = []
    vectors = []
    for first_idx in range(degree):
        entries = []
        basis_row = []
        for second_idx in range(degree):
            if first_idx == second_idx:
                entries.append(alpha_list[first_idx])
                basis_row.append(ones_row)
            elif abs(first_idx - second_idx) == 1:
                entries.append(beta_list[min(first_idx, second_idx)])
                basis_row.append(zeros_row)
            else:
                entries.append(zeros_row)
                basis_row.append(zeros_row)
        matrix.append(entries)
        vectors.append(basis_row)
    for sweep_index in range(jacobi_sweeps):
        for first_idx in range(degree):
            for second_idx in range(first_idx + 1, degree):
                coupling = matrix[first_idx][second_idx]
                rotate_by = 0.5 * jnp.arctan2(2.0 * coupling, matrix[second_idx][second_idx] - matrix[first_idx][first_idx])
                cosine = jnp.cos(rotate_by)
                sine_val = jnp.sin(rotate_by)
                for row_idx in range(degree):
                    left_val = matrix[row_idx][first_idx]
                    right_val = matrix[row_idx][second_idx]
                    matrix[row_idx][first_idx] = cosine * left_val - sine_val * right_val
                    matrix[row_idx][second_idx] = sine_val * left_val + cosine * right_val
                    left_vec = vectors[row_idx][first_idx]
                    right_vec = vectors[row_idx][second_idx]
                    vectors[row_idx][first_idx] = cosine * left_vec - sine_val * right_vec
                    vectors[row_idx][second_idx] = sine_val * left_vec + cosine * right_vec
                for col_idx in range(degree):
                    upper_val = matrix[first_idx][col_idx]
                    lower_val = matrix[second_idx][col_idx]
                    matrix[first_idx][col_idx] = cosine * upper_val - sine_val * lower_val
                    matrix[second_idx][col_idx] = sine_val * upper_val + cosine * lower_val
    total = zeros_row
    for index_k in range(degree):
        total = total + vectors[0][index_k] * vectors[0][index_k] * jnp.log(matrix[index_k][index_k])
    return total

def reference(points, inverse_scales, probe_signs):
    scaled = points * inverse_scales[:, None]
    direction = 2.0 * probe_signs.astype(jnp.float32) - 1.0
    basis_prev = jnp.zeros_like(direction)
    alpha_list = []
    beta_list = []
    for lanczos_step in range(STEPS):
        squares = lax.optimization_barrier(jnp.sum(direction * direction, axis=0))
        image = apply_kernel(scaled, direction.astype(jnp.bfloat16)) + noise_level * direction
        curvature = lax.optimization_barrier(jnp.sum(direction * image, axis=0))
        beta_now = jnp.sqrt(squares + epsilon)
        alpha_now = curvature / (beta_now * beta_now)
        alpha_list.append(alpha_now)
        beta_list.append(beta_now)
        if lanczos_step + 1 < STEPS:
            basis_now = direction / beta_now
            direction = image / beta_now - alpha_now * basis_now - beta_now * basis_prev
            basis_prev = basis_now
    logdet_terms = log_weight(alpha_list, beta_list[1:])
    return (alpha_list[0], logdet_terms)
```

```python
import functools
import math

import jax
import jax.numpy as jnp
from jax import lax
from jax.experimental import pallas as pl
from jax.experimental.pallas import tpu as pltpu
from jax.sharding import Mesh
from jax.sharding import PartitionSpec as P

AXES = ("x_lo", "z", "x_hi", "y", "core")
ROW = ("x_lo", "z")
COL = ("x_hi", "y")

N = 32768
DIM = 16
PIECE = 256
PROBES = 128
GROUP = 8
BLOCK = GROUP * PIECE
FEATURES = 128
TAIL = 16
ROWS = PIECE + TAIL

epsilon = 1e-06
noise_level = 1.0
jacobi_sweeps = 6

BETA_1 = math.sqrt(N + epsilon)
SHIFT_1 = 2.0
SHIFT_2 = 2.0

bf16 = jnp.bfloat16
f32 = jnp.float32

PARAMS = pltpu.CompilerParams(vmem_limit_bytes=48 * 2**20)


def call(body, outs, *args, scratch=(), flops=0, **kw):
    whole = pl.BlockSpec(memory_space=pltpu.VMEM)
    single = not isinstance(outs[1], tuple)
    outs = (outs,) if single else outs
    result = pl.pallas_call(
        body,
        out_shape=tuple(jax.ShapeDtypeStruct(s, d) for s, d in outs),
        in_specs=[whole] * len(args),
        out_specs=tuple([whole] * len(outs)),
        scratch_shapes=list(scratch),
        compiler_params=PARAMS,
        **kw,
    )(*args)
    return result[0] if single else result


def parts(value):
    high = value.astype(bf16)
    rest = value - high.astype(f32)
    middle = rest.astype(bf16)
    low = (rest - middle.astype(f32)).astype(bf16)
    return high, middle, low


def prepare(points_ref, scales_ref, signs_ref, send_ref, right_ref, direction_ref):
    scaled = points_ref[...] * scales_ref[...] * math.sqrt(math.log2(math.e))
    norms = -0.5 * jnp.sum(scaled * scaled, axis=0, keepdims=True)
    high, middle, low = parts(scaled)
    row = lax.broadcasted_iota(jnp.int32, (TAIL, PIECE), 0)
    pieces = [jnp.broadcast_to(p.astype(f32), (TAIL, PIECE)) for p in parts(norms)]
    one = jnp.ones((TAIL, PIECE), f32)
    zero = jnp.zeros((TAIL, PIECE), f32)

    def rows(values):
        block = zero
        for place, value in enumerate(values):
            block = jnp.where(row == place, value, block)
        return block.astype(bf16)

    left_norms = rows(pieces + [one] * 3)
    right_norms = rows([one] * 3 + pieces)
    direction = 2.0 * signs_ref[...].astype(f32) - 1.0
    direction_ref[...] = direction
    half = direction.astype(bf16)
    for dest in range(GROUP):
        send_ref[dest, :PIECE] = half
        for side in range(2):
            cut = slice(side * 128, side * 128 + 128)
            for place, value in enumerate((high, middle, low)):
                base = side * 64 + place * 16
                send_ref[dest, PIECE + base : PIECE + base + 16] = value[:, cut]
                right_ref[dest, base : base + 16] = value[:, cut]
            base = side * 64 + 48
            send_ref[dest, PIECE + base : PIECE + base + 16] = left_norms[:, cut]
            right_ref[dest, base : base + 16] = right_norms[:, cut]


def features(read, order, out_ref):
    for piece in range(GROUP):
        for side in range(2):
            cut = slice(piece * PIECE + side * 128, piece * PIECE + side * 128 + 128)
            for place, part in enumerate(order):
                base = side * 64 + part * 16
                out_ref[place * 16 : place * 16 + 16, cut] = read(piece, base)
    out_ref[112:128, :] = jnp.zeros((16, BLOCK), bf16)


def evaluate(first, *refs):
    if first:
        recv_ref, right_ref, kernel_ref, out_ref, left, right = refs
    else:
        recv_ref, right_ref, before_ref, kernel_ref, out_ref, left, right = refs
    features(lambda p, b: recv_ref[p, PIECE + b : PIECE + b + 16, :], (0, 0, 1, 0, 2, 1, 3), left)
    features(lambda p, b: right_ref[p, b : b + 16, :], (0, 1, 0, 2, 0, 1, 3), right)
    width = 512

    def tile(step, carry):
        rows = pl.ds(pl.multiple_of(step * PIECE, PIECE), PIECE)
        mine = right[:, rows].T
        total = None if first else before_ref[step]
        for at in range(0, BLOCK, width):
            power = jnp.dot(mine, left[:, at : at + width], preferred_element_type=f32)
            kernel = jnp.exp2(jnp.minimum(power, 0.0)).astype(bf16)
            kernel_ref[rows, at : at + width] = kernel
            half = recv_ref[at // PIECE : (at + width) // PIECE, :PIECE, :].reshape(width, PROBES)
            product = jnp.dot(kernel, half, preferred_element_type=f32)
            total = product if total is None else total + product
        out_ref[step] = total.astype(out_ref.dtype)
        return carry

    lax.fori_loop(0, GROUP, tile, 0)


def multiply(kernel_ref, half, step):
    rows = pl.ds(pl.multiple_of(step * PIECE, PIECE), PIECE)
    return jnp.dot(kernel_ref[rows, :], half, preferred_element_type=f32)


def multiply_first(kernel_ref, recv_ref, out_ref):
    half = recv_ref[:, :PIECE, :].reshape(BLOCK, PROBES)

    def tile(step, carry):
        out_ref[step] = multiply(kernel_ref, half, step)
        return carry

    lax.fori_loop(0, GROUP, tile, 0)


def tail_sums(refs, count):
    sums = []
    for scalar in range(count):
        total = jnp.zeros((1, PROBES), f32)
        for ref in refs:
            tail = ref[:, PIECE:ROWS, :].astype(f32)
            total = total + jnp.sum(
                jnp.sum(tail[:, 3 * scalar : 3 * scalar + 3], axis=1, keepdims=True), axis=0
            )
        sums.append(total)
    return sums


def tail_rows(values):
    row = lax.broadcasted_iota(jnp.int32, (TAIL, PROBES), 0)
    block = jnp.zeros((TAIL, PROBES), f32)
    for scalar, value in enumerate(values):
        for place, part in enumerate(parts(value)):
            block = jnp.where(
                row == 3 * scalar + place, jnp.broadcast_to(part.astype(f32), block.shape), block
            )
    return block.astype(bf16)


def multiply_second(kernel_ref, before_ref, mine_ref, recv_ref, out_ref):
    half = recv_ref[:, :PIECE, :].reshape(BLOCK, PROBES)
    tail = tail_rows(tail_sums((mine_ref, recv_ref), 2))

    def tile(step, carry):
        total = before_ref[step] + multiply(kernel_ref, half, step)
        out_ref[step, :PIECE] = total.astype(bf16)
        out_ref[step, PIECE:] = tail
        return carry

    lax.fori_loop(0, GROUP, tile, 0)


def column_sum(value):
    return jnp.sum(value, axis=0, keepdims=True)


def after_first(recv_ref, direction_ref, image_ref, send_ref):
    product = jnp.sum(recv_ref[...].astype(f32), axis=0)
    direction = direction_ref[...]
    shifted = product + (noise_level - SHIFT_1) * direction
    image_ref[...] = product
    tail = tail_rows([column_sum(direction * shifted), column_sum(shifted * shifted)])
    half = shifted.astype(bf16)
    for dest in range(GROUP):
        send_ref[dest, :PIECE] = half
        send_ref[dest, PIECE:] = tail


def after_second(recv_ref, direction_ref, image_ref, send_ref, known_ref):
    along, square = tail_sums((recv_ref,), 2)
    product = jnp.sum(recv_ref[:, :PIECE, :].astype(f32), axis=0)
    direction, image = direction_ref[...], image_ref[...]
    scale = BETA_1 * BETA_1
    alpha_1 = (along + SHIFT_1 * N) / scale
    excess = alpha_1 - SHIFT_1
    squares_2 = jnp.maximum(square - 2.0 * excess * along + excess * excess * N, 0.0) / scale
    beta_2 = jnp.sqrt(squares_2 + epsilon)
    shifted = image + (noise_level - SHIFT_1) * direction
    second = (shifted - excess * direction) * (1.0 / BETA_1)
    moved = (product - excess * image) * (1.0 / BETA_1)
    third = (moved + (noise_level - SHIFT_2) * second) / beta_2 - beta_2 * (
        direction * (1.0 / BETA_1)
    )
    known_ref[...] = jnp.concatenate([alpha_1, beta_2] + [jnp.zeros((6, PROBES), f32)], axis=0)
    tail = tail_rows(
        [
            column_sum(second * moved),
            column_sum(third * third),
            column_sum(third * second),
            column_sum(third * moved),
            column_sum(second * second),
        ]
    )
    half = third.astype(bf16)
    for dest in range(GROUP):
        send_ref[dest, :PIECE] = half
        send_ref[dest, PIECE:] = tail


def tails(mine_ref, other_ref, own_ref, send_ref):
    tail = tail_rows(tail_sums((mine_ref, other_ref), 5))
    half = own_ref[0, :PIECE, :]
    for dest in range(GROUP):
        send_ref[dest, :PIECE] = half
        send_ref[dest, PIECE:] = tail


def multiply_last(kernel_ref, before_ref, recv_ref, right_ref, known_ref, out_ref, sums_ref):
    half = recv_ref[:, :PIECE, :].reshape(BLOCK, PROBES)

    def tile(step, carry):
        total = before_ref[step] + multiply(kernel_ref, half, step)
        return carry + column_sum(right_ref[step, :PIECE, :].astype(f32) * total)

    quad = lax.fori_loop(0, GROUP, tile, jnp.zeros((1, PROBES), f32))
    out_ref[...] = jnp.broadcast_to(quad[:, None, :], out_ref.shape)
    sums = tail_sums((right_ref,), 5)
    sums_ref[...] = jnp.concatenate(sums + [jnp.zeros((3, PROBES), f32)], axis=0)


def log_weight(alpha_list, beta_list):
    degree = len(alpha_list)
    zeros_row = jnp.zeros(alpha_list[0].shape, f32)
    ones_row = jnp.ones(alpha_list[0].shape, f32)
    matrix = [[zeros_row] * degree for _ in range(degree)]
    vectors = [[zeros_row] * degree for _ in range(degree)]
    for idx in range(degree):
        matrix[idx][idx] = alpha_list[idx]
        vectors[idx][idx] = ones_row
        if idx + 1 < degree:
            matrix[idx][idx + 1] = beta_list[idx]
            matrix[idx + 1][idx] = beta_list[idx]
    for _ in range(jacobi_sweeps):
        for p in range(degree):
            for q in range(p + 1, degree):
                rotate_by = 0.5 * jnp.arctan2(2.0 * matrix[p][q], matrix[q][q] - matrix[p][p])
                cosine = jnp.cos(rotate_by)
                sine = jnp.sin(rotate_by)
                for grid in (matrix, vectors):
                    for row in grid:
                        left, right = row[p], row[q]
                        row[p] = cosine * left - sine * right
                        row[q] = sine * left + cosine * right
                for col in range(degree):
                    upper, lower = matrix[p][col], matrix[q][col]
                    matrix[p][col] = cosine * upper - sine * lower
                    matrix[q][col] = sine * upper + cosine * lower
    total = zeros_row
    for k in range(degree):
        total = total + vectors[0][k] * vectors[0][k] * jnp.log(matrix[k][k])
    return total


def swap_cores(value):
    return lax.ppermute(value, "core", [(0, 1), (1, 0)])


def exchange(value, axes):
    return lax.all_to_all(value, axes, 0, 0, tiled=True)


def per_device(points, inverse_scales, probe_signs):
    piece = ((PIECE, PROBES), f32)
    padded = ((GROUP, ROWS, PROBES), bf16)
    block = ((GROUP, PIECE, PROBES), f32)
    kernel_half = ((BLOCK, BLOCK), bf16)
    scratch = [pltpu.VMEM((FEATURES, BLOCK), bf16), pltpu.VMEM((FEATURES, BLOCK), bf16)]
    send, right, direction = call(
        prepare,
        (((GROUP, PIECE + 128, PROBES), bf16), ((GROUP, 128, PROBES), bf16), piece),
        points,
        inverse_scales[:, None],
        probe_signs,
    )
    right = exchange(right, ROW)
    mine = exchange(send, COL)
    other = swap_cores(mine)
    kernel_mine, total = call(
        functools.partial(evaluate, True), (kernel_half, block), mine, right, scratch=scratch
    )
    kernel_other, total = call(
        functools.partial(evaluate, False),
        (kernel_half, ((GROUP, PIECE, PROBES), bf16)),
        other,
        right,
        total,
        scratch=scratch,
    )
    recv = exchange(total, ROW)
    image, send = call(after_first, (piece, padded), recv, direction)
    mine = exchange(send, COL)
    other = swap_cores(mine)
    total = call(multiply_first, block, kernel_mine, mine)
    send = call(multiply_second, padded, kernel_other, total, mine, other)
    recv = exchange(send, ROW)
    own, known = call(after_second, (padded, ((8, PROBES), f32)), recv, direction, image)
    mine = exchange(own, COL)
    other = swap_cores(mine)
    send = call(tails, padded, mine, other, own)
    right = exchange(send, ROW)
    total = call(multiply_first, block, kernel_mine, mine)
    quad, sums = call(
        multiply_last,
        (((128, 1, PROBES), f32), ((8, PROBES), f32)),
        kernel_other,
        total,
        other,
        right,
        known,
    )
    quad = jnp.sum(exchange(quad, AXES), axis=(0, 1))
    alpha_1, beta_2 = known[0], known[1]
    scale = beta_2 * beta_2
    alpha_2 = (sums[0] + noise_level * sums[4]) / scale
    turn = (alpha_2 - SHIFT_2) / beta_2
    squares_3 = jnp.maximum(sums[1] - 2.0 * turn * sums[2] + turn * turn * sums[4], 0.0)
    curvature_3 = quad - 2.0 * turn * sums[3] + turn * turn * sums[0] + noise_level * squares_3
    beta_3 = jnp.sqrt(squares_3 + epsilon)
    alpha_3 = curvature_3 / (beta_3 * beta_3)
    return alpha_1, log_weight([alpha_1, alpha_2, alpha_3], [beta_2, beta_3])


def solution(mesh):
    split = Mesh(mesh.devices.reshape(2, 4, 2, 4, 2), AXES)
    return jax.shard_map(
        per_device,
        mesh=split,
        in_specs=(P(None, AXES), P(), P(AXES, None)),
        out_specs=(P(), P()),
        check_vma=False,
    )
```

```python
import math

import jax
import jax.numpy as jnp
from jax import lax
from jax.experimental import pallas as pl
from jax.experimental.pallas import tpu as pltpu
from jax.sharding import Mesh
from jax.sharding import PartitionSpec as P

AXES = ("x_lo", "z", "x_hi", "y", "core")
ROW = ("x_lo", "z")
COL = ("x_hi", "y")

N = 32768
DIM = 16
PIECE = 256
PROBES = 128
GROUP = 8
BLOCK = GROUP * PIECE
FEATURES = 128
TAIL = 16

epsilon = 1e-06
noise_level = 1.0
jacobi_sweeps = 6

BETA_1 = math.sqrt(N + epsilon)
SHIFT_1 = 2.0
SHIFT_2 = 2.0

bf16 = jnp.bfloat16
f32 = jnp.float32

PARAMS = pltpu.CompilerParams(vmem_limit_bytes=24 * 2**20)


def resident(shape, dtype):
    return pltpu.VMEM(shape, dtype)


def call(body, outs, *args, scratch=(), in_specs=None):
    whole = pl.BlockSpec(memory_space=pltpu.VMEM)
    return pl.pallas_call(
        body,
        out_shape=tuple(outs),
        in_specs=in_specs or [whole] * len(args),
        out_specs=tuple([whole] * len(outs)),
        scratch_shapes=list(scratch),
        compiler_params=PARAMS,
    )(*args)


def parts(value):
    high = value.astype(bf16)
    rest = value - high.astype(f32)
    middle = rest.astype(bf16)
    low = (rest - middle.astype(f32)).astype(bf16)
    return high, middle, low


def stack_rows(values, shape):
    row = lax.broadcasted_iota(jnp.int32, shape, 0)
    block = jnp.zeros(shape, f32)
    for place, value in enumerate(values):
        block = jnp.where(row == place, jnp.broadcast_to(value, shape), block)
    return block


def as_rows(columns):
    lane = lax.broadcasted_iota(jnp.int32, (PROBES, PROBES), 1)
    block = jnp.zeros((PROBES, PROBES), f32)
    for place, value in enumerate(columns):
        block = jnp.where(lane == place, value, block)
    block = block.T
    return [block[place : place + 1] for place in range(len(columns))]


def as_columns(rows):
    block = stack_rows(rows, (PROBES, PROBES)).T
    return [block[:, place : place + 1] for place in range(len(rows))]


def lane_sum(value):
    return jnp.sum(value, axis=1, keepdims=True)


def tail_rows(rows):
    values = [part.astype(f32) for row in rows for part in parts(row)]
    block = stack_rows(values, (TAIL, PROBES))
    return jnp.concatenate([block, jnp.zeros_like(block)], axis=1).astype(bf16)


def tail_sums(refs, count):
    total = jnp.zeros((TAIL, PROBES), f32)
    for ref in refs:
        for piece in range(GROUP):
            total = total + ref[piece, PROBES:, :PROBES].astype(f32)
    return [
        total[3 * k : 3 * k + 1] + total[3 * k + 1 : 3 * k + 2] + total[3 * k + 2 : 3 * k + 3]
        for k in range(count)
    ]


def prepare(
    points_hbm,
    scales_hbm,
    signs_hbm,
    send_ref,
    right_ref,
    direction_ref,
    points_ref,
    scales_ref,
    signs_ref,
    sems,
):
    copies = [
        pltpu.make_async_copy(src, dst, sems.at[i])
        for i, (src, dst) in enumerate(
            ((points_hbm, points_ref), (scales_hbm, scales_ref), (signs_hbm, signs_ref))
        )
    ]
    for copy in copies:
        copy.start()
    for copy in copies:
        copy.wait()
    square = (DIM, DIM)
    same = lax.broadcasted_iota(jnp.int32, square, 0) == lax.broadcasted_iota(jnp.int32, square, 1)
    scales = lane_sum(jnp.where(same, jnp.broadcast_to(scales_ref[...], square), 0.0))
    scaled = points_ref[...] * scales * math.sqrt(math.log2(math.e))
    norms = -0.5 * jnp.sum(scaled * scaled, axis=0, keepdims=True)
    pieces = [part.astype(f32) for part in parts(norms)]
    one = jnp.ones((1, PIECE), f32)
    shape = (16, PIECE)
    points = list(parts(scaled))
    left = jnp.concatenate(points + [stack_rows(pieces + [one] * 3, shape).astype(bf16)], axis=0)
    right = jnp.concatenate(points + [stack_rows([one] * 3 + pieces, shape).astype(bf16)], axis=0)
    direction = (2.0 * signs_ref[...].astype(f32) - 1.0).T
    direction_ref[...] = direction
    half = direction.astype(bf16)
    for dest in range(GROUP):
        send_ref[dest, :PROBES] = half
        send_ref[dest, PROBES:] = left
        right_ref[dest] = right


def features(read, order):
    rows = [read(16 * part) for part in order]
    return jnp.concatenate(rows + [jnp.zeros((16, PIECE), bf16)], axis=0)


def wide(ref):
    return jnp.concatenate([ref[piece, :PROBES, :] for piece in range(GROUP)], axis=1)


def span(piece):
    return slice(piece * PIECE, (piece + 1) * PIECE)


def evaluate(recv_ref, right_ref, kernel_ref, left, right):
    for piece in range(GROUP):
        left[span(piece), :] = features(
            lambda b: recv_ref[piece, PROBES + b : PROBES + b + 16, :], (0, 0, 1, 0, 2, 1, 3)
        ).T
        right[:, span(piece)] = features(
            lambda b: right_ref[piece, b : b + 16, :], (0, 1, 0, 2, 0, 1, 3)
        )

    def tile(step, carry):
        rows = pl.ds(pl.multiple_of(step * 512, 512), 512)
        for piece in range(GROUP):
            power = jnp.dot(left[rows, :], right[:, span(piece)], preferred_element_type=f32)
            kernel_ref[rows, span(piece)] = jnp.exp2(jnp.minimum(power, 0.0)).astype(bf16)
        return carry

    lax.fori_loop(0, BLOCK // 512, tile, 0)


def evaluate_first(recv_ref, right_ref, kernel_ref, out_ref, left, right):
    evaluate(recv_ref, right_ref, kernel_ref, left, right)
    out_ref[...] = multiply(kernel_ref, recv_ref)


def evaluate_second(recv_ref, right_ref, before_ref, kernel_ref, out_ref, left, right):
    evaluate(recv_ref, right_ref, kernel_ref, left, right)
    total = before_ref[...] + multiply(kernel_ref, recv_ref)
    for piece in range(GROUP):
        out_ref[piece] = total[:, span(piece)].astype(bf16)


def multiply(kernel_ref, recv_ref):
    return jnp.dot(wide(recv_ref), kernel_ref[...], preferred_element_type=f32)


def multiply_first(kernel_ref, recv_ref, out_ref):
    out_ref[...] = multiply(kernel_ref, recv_ref)


def multiply_second(kernel_ref, before_ref, mine_ref, recv_ref, out_ref):
    total = before_ref[...] + multiply(kernel_ref, recv_ref)
    tail = tail_rows(tail_sums((mine_ref, recv_ref), 2))
    for piece in range(GROUP):
        out_ref[piece, :PROBES] = total[:, span(piece)].astype(bf16)
        out_ref[piece, PROBES:] = tail


def total_of(recv_ref):
    total = recv_ref[0, :PROBES, :].astype(f32)
    for piece in range(1, GROUP):
        total = total + recv_ref[piece, :PROBES, :].astype(f32)
    return total


def send_all(send_ref, vector, tail):
    for dest in range(GROUP):
        send_ref[dest, :PROBES] = vector
        send_ref[dest, PROBES:] = tail


def after_first(recv_ref, direction_ref, image_ref, send_ref):
    product = total_of(recv_ref)
    direction = direction_ref[...]
    shifted = product + (noise_level - SHIFT_1) * direction
    image_ref[...] = product
    sums = as_rows([lane_sum(direction * shifted), lane_sum(shifted * shifted)])
    send_all(send_ref, shifted.astype(bf16), tail_rows(sums))


def after_second(recv_ref, direction_ref, image_ref, send_ref, known_ref):
    along, square = tail_sums((recv_ref,), 2)
    scale = BETA_1 * BETA_1
    alpha_1 = (along + SHIFT_1 * N) / scale
    excess = alpha_1 - SHIFT_1
    squares_2 = jnp.maximum(square - 2.0 * excess * along + excess * excess * N, 0.0) / scale
    beta_2 = jnp.sqrt(squares_2 + epsilon)
    known_ref[...] = stack_rows([alpha_1, beta_2], (8, PROBES))
    excess, over, beta = as_columns([excess, 1.0 / beta_2, beta_2 * (1.0 / BETA_1)])
    product = total_of(recv_ref)
    direction, image = direction_ref[...], image_ref[...]
    shifted = image + (noise_level - SHIFT_1) * direction
    second = (shifted - excess * direction) * (1.0 / BETA_1)
    moved = (product - excess * image) * (1.0 / BETA_1)
    third = (moved + (noise_level - SHIFT_2) * second) * over - beta * direction
    sums = as_rows(
        [
            lane_sum(second * moved),
            lane_sum(third * third),
            lane_sum(third * second),
            lane_sum(third * moved),
            lane_sum(second * second),
        ]
    )
    send_all(send_ref, third.astype(bf16), tail_rows(sums))


def tails(mine_ref, other_ref, own_ref, send_ref):
    send_all(send_ref, own_ref[0, :PROBES, :], tail_rows(tail_sums((mine_ref, other_ref), 5)))


def multiply_last(kernel_ref, before_ref, recv_ref, right_ref, out_ref, sums_ref):
    total = before_ref[...] + multiply(kernel_ref, recv_ref)
    (quad,) = as_rows([lane_sum(wide(right_ref).astype(f32) * total)])
    out_ref[...] = jnp.broadcast_to(quad[None], out_ref.shape)
    sums_ref[...] = stack_rows(tail_sums((right_ref,), 5), (8, PROBES))


def log_weight(alpha_list, beta_list):
    degree = len(alpha_list)
    zeros_row = jnp.zeros(alpha_list[0].shape, f32)
    ones_row = jnp.ones(alpha_list[0].shape, f32)
    matrix = [[zeros_row] * degree for _ in range(degree)]
    vectors = [[zeros_row] * degree for _ in range(degree)]
    for idx in range(degree):
        matrix[idx][idx] = alpha_list[idx]
        vectors[idx][idx] = ones_row
        if idx + 1 < degree:
            matrix[idx][idx + 1] = beta_list[idx]
            matrix[idx + 1][idx] = beta_list[idx]
    for _ in range(jacobi_sweeps):
        for p in range(degree):
            for q in range(p + 1, degree):
                rotate_by = 0.5 * jnp.arctan2(2.0 * matrix[p][q], matrix[q][q] - matrix[p][p])
                cosine = jnp.cos(rotate_by)
                sine = jnp.sin(rotate_by)
                for grid in (matrix, vectors):
                    for row in grid:
                        left, right = row[p], row[q]
                        row[p] = cosine * left - sine * right
                        row[q] = sine * left + cosine * right
                for col in range(degree):
                    upper, lower = matrix[p][col], matrix[q][col]
                    matrix[p][col] = cosine * upper - sine * lower
                    matrix[q][col] = sine * upper + cosine * lower
    total = zeros_row
    for k in range(degree):
        total = total + vectors[0][k] * vectors[0][k] * jnp.log(matrix[k][k])
    return total


def swap_cores(value):
    return lax.ppermute(value, "core", [(0, 1), (1, 0)])


def exchange(value, axes):
    return lax.all_to_all(value, axes, 0, 0, tiled=True)


def per_device(points, inverse_scales, probe_signs):
    piece = resident((PROBES, PIECE), f32)
    padded = resident((GROUP, PROBES + TAIL, PIECE), bf16)
    block = resident((PROBES, BLOCK), f32)
    kernel_half = resident((BLOCK, BLOCK), bf16)
    scratch = [pltpu.VMEM((BLOCK, FEATURES), bf16), pltpu.VMEM((FEATURES, BLOCK), bf16)]
    send, right, direction = call(
        prepare,
        (
            resident((GROUP, PROBES + 64, PIECE), bf16),
            resident((GROUP, 64, PIECE), bf16),
            piece,
        ),
        points,
        inverse_scales[None],
        probe_signs,
        in_specs=[pl.BlockSpec(memory_space=pltpu.HBM)] * 3,
        scratch=[
            pltpu.VMEM((DIM, PIECE), f32),
            pltpu.VMEM((1, DIM), f32),
            pltpu.VMEM((PIECE, PROBES), jnp.int32),
            pltpu.SemaphoreType.DMA((3,)),
        ],
    )
    mine = exchange(send, COL)
    other = swap_cores(mine)
    right = exchange(right, ROW)
    kernel_mine, total = call(evaluate_first, (kernel_half, block), mine, right, scratch=scratch)
    kernel_other, total = call(
        evaluate_second,
        (kernel_half, resident((GROUP, PROBES, PIECE), bf16)),
        other,
        right,
        total,
        scratch=scratch,
    )
    recv = exchange(total, ROW)
    image, send = call(after_first, (piece, padded), recv, direction)
    mine = exchange(send, COL)
    other = swap_cores(mine)
    (total,) = call(multiply_first, (block,), kernel_mine, mine)
    (send,) = call(multiply_second, (padded,), kernel_other, total, mine, other)
    recv = exchange(send, ROW)
    own, known = call(
        after_second, (padded, resident((8, PROBES), f32)), recv, direction, image
    )
    mine = exchange(own, COL)
    other = swap_cores(mine)
    (send,) = call(tails, (padded,), mine, other, own)
    right = exchange(send, ROW)
    (total,) = call(multiply_first, (block,), kernel_mine, mine)
    quad, sums = call(
        multiply_last,
        (resident((128, 1, PROBES), f32), resident((8, PROBES), f32)),
        kernel_other,
        total,
        other,
        right,
    )
    quad = jnp.sum(exchange(quad, AXES), axis=(0, 1))
    alpha_1, beta_2 = known[0], known[1]
    scale = beta_2 * beta_2
    alpha_2 = (sums[0] + noise_level * sums[4]) / scale
    turn = (alpha_2 - SHIFT_2) / beta_2
    squares_3 = jnp.maximum(sums[1] - 2.0 * turn * sums[2] + turn * turn * sums[4], 0.0)
    curvature_3 = quad - 2.0 * turn * sums[3] + turn * turn * sums[0] + noise_level * squares_3
    beta_3 = jnp.sqrt(squares_3 + epsilon)
    alpha_3 = curvature_3 / (beta_3 * beta_3)
    return alpha_1, log_weight([alpha_1, alpha_2, alpha_3], [beta_2, beta_3])


def solution(mesh):
    split = Mesh(mesh.devices.reshape(2, 4, 2, 4, 2), AXES)
    return jax.shard_map(
        per_device,
        mesh=split,
        in_specs=(P(None, AXES), P(), P(AXES, None)),
        out_specs=(P(), P()),
        check_vma=False,
    )
```

```python
import math

import jax
import jax.numpy as jnp
from jax import lax
from jax.experimental import pallas as pl
from jax.experimental.pallas import tpu as pltpu
from jax.sharding import Mesh
from jax.sharding import PartitionSpec as P

AXES = ("x_lo", "z", "x_hi", "y", "core")
ROW = ("x_lo", "z")
COL = ("x_hi", "y")

N = 32768
DIM = 16
PIECE = 256
PROBES = 128
GROUP = 8
BLOCK = GROUP * PIECE
FEATURES = 128
TAIL = 16

epsilon = 1e-06
noise_level = 1.0
jacobi_sweeps = 6

BETA_1 = math.sqrt(N + epsilon)
SHIFT_1 = 2.0
SHIFT_2 = 2.0

bf16 = jnp.bfloat16
f32 = jnp.float32


def resident(shape, dtype):
    return pltpu.VMEM(shape, dtype)


def call(body, outs, *args, scratch=(), in_specs=None, limit=12):
    whole = pl.BlockSpec(memory_space=pltpu.VMEM)
    return pl.pallas_call(
        body,
        out_shape=tuple(outs),
        in_specs=in_specs or [whole] * len(args),
        out_specs=tuple([whole] * len(outs)),
        scratch_shapes=list(scratch),
        compiler_params=pltpu.CompilerParams(vmem_limit_bytes=limit * 2**20),
    )(*args)


def parts(value):
    high = value.astype(bf16)
    rest = value - high.astype(f32)
    middle = rest.astype(bf16)
    low = (rest - middle.astype(f32)).astype(bf16)
    return high, middle, low


def stack_rows(values, shape):
    row = lax.broadcasted_iota(jnp.int32, shape, 0)
    block = jnp.zeros(shape, f32)
    for place, value in enumerate(values):
        block = jnp.where(row == place, jnp.broadcast_to(value, shape), block)
    return block


def as_rows(columns):
    lane = lax.broadcasted_iota(jnp.int32, (PROBES, PROBES), 1)
    block = jnp.zeros((PROBES, PROBES), f32)
    for place, value in enumerate(columns):
        block = jnp.where(lane == place, value, block)
    block = block.T
    return [block[place : place + 1] for place in range(len(columns))]


def as_columns(rows):
    block = stack_rows(rows, (PROBES, PROBES)).T
    return [block[:, place : place + 1] for place in range(len(rows))]


def lane_sum(value):
    return jnp.sum(value, axis=1, keepdims=True)


def tail_rows(rows):
    values = [part.astype(f32) for row in rows for part in parts(row)]
    block = stack_rows(values, (TAIL, PROBES))
    return jnp.concatenate([block, jnp.zeros_like(block)], axis=1).astype(bf16)


def tail_sums(refs, count):
    total = jnp.zeros((TAIL, PROBES), f32)
    for ref in refs:
        for piece in range(GROUP):
            total = total + ref[piece, PROBES:, :PROBES].astype(f32)
    return [
        total[3 * k : 3 * k + 1] + total[3 * k + 1 : 3 * k + 2] + total[3 * k + 2 : 3 * k + 3]
        for k in range(count)
    ]


def prepare(
    points_hbm,
    scales_hbm,
    signs_hbm,
    send_ref,
    right_ref,
    direction_ref,
    points_ref,
    scales_ref,
    signs_ref,
    sems,
):
    copies = [
        pltpu.make_async_copy(src, dst, sems.at[i])
        for i, (src, dst) in enumerate(
            ((points_hbm, points_ref), (scales_hbm, scales_ref), (signs_hbm, signs_ref))
        )
    ]
    for copy in copies:
        copy.start()
    for copy in copies:
        copy.wait()
    square = (DIM, DIM)
    same = lax.broadcasted_iota(jnp.int32, square, 0) == lax.broadcasted_iota(jnp.int32, square, 1)
    scales = lane_sum(jnp.where(same, jnp.broadcast_to(scales_ref[...], square), 0.0))
    scaled = points_ref[...] * scales * math.sqrt(math.log2(math.e))
    norms = -0.5 * jnp.sum(scaled * scaled, axis=0, keepdims=True)
    pieces = [part.astype(f32) for part in parts(norms)]
    one = jnp.ones((1, PIECE), f32)
    shape = (16, PIECE)
    points = list(parts(scaled))
    left = jnp.concatenate(points + [stack_rows(pieces + [one] * 3, shape).astype(bf16)], axis=0)
    right = jnp.concatenate(points + [stack_rows([one] * 3 + pieces, shape).astype(bf16)], axis=0)
    direction = (2.0 * signs_ref[...].astype(f32) - 1.0).T
    direction_ref[...] = direction
    half = direction.astype(bf16)
    for dest in range(GROUP):
        send_ref[dest, :PROBES] = half
        send_ref[dest, PROBES:] = left
        right_ref[dest] = right


def features(read, order):
    rows = [read(16 * part) for part in order]
    return jnp.concatenate(rows + [jnp.zeros((16, PIECE), bf16)], axis=0)


def wide(ref):
    return jnp.concatenate([ref[piece, :PROBES, :] for piece in range(GROUP)], axis=1)


def span(piece):
    return slice(piece * PIECE, (piece + 1) * PIECE)


def evaluate(recv_ref, right_ref, kernel_ref, left, right):
    for piece in range(GROUP):
        left[span(piece), :] = features(
            lambda b: recv_ref[piece, PROBES + b : PROBES + b + 16, :], (0, 0, 1, 0, 2, 1, 3)
        ).T
        right[:, span(piece)] = features(
            lambda b: right_ref[piece, b : b + 16, :], (0, 1, 0, 2, 0, 1, 3)
        )

    def tile(step, carry):
        rows = pl.ds(pl.multiple_of(step * 512, 512), 512)
        for piece in range(GROUP):
            power = jnp.dot(left[rows, :], right[:, span(piece)], preferred_element_type=f32)
            kernel_ref[rows, span(piece)] = jnp.exp2(jnp.minimum(power, 0.0)).astype(bf16)
        return carry

    lax.fori_loop(0, BLOCK // 512, tile, 0)


def evaluate_first(recv_ref, right_ref, kernel_ref, out_ref, left, right):
    evaluate(recv_ref, right_ref, kernel_ref, left, right)
    out_ref[...] = multiply(kernel_ref, recv_ref)


def evaluate_second(recv_ref, right_ref, before_ref, kernel_ref, out_ref, left, right):
    evaluate(recv_ref, right_ref, kernel_ref, left, right)
    total = before_ref[...] + multiply(kernel_ref, recv_ref)
    for piece in range(GROUP):
        out_ref[piece] = total[:, span(piece)].astype(bf16)


def multiply(kernel_ref, recv_ref):
    return jnp.dot(wide(recv_ref), kernel_ref[...], preferred_element_type=f32)


def multiply_first(kernel_ref, recv_ref, out_ref):
    out_ref[...] = multiply(kernel_ref, recv_ref)


def multiply_second(kernel_ref, before_ref, mine_ref, recv_ref, out_ref):
    total = before_ref[...] + multiply(kernel_ref, recv_ref)
    tail = tail_rows(tail_sums((mine_ref, recv_ref), 2))
    for piece in range(GROUP):
        out_ref[piece, :PROBES] = total[:, span(piece)].astype(bf16)
        out_ref[piece, PROBES:] = tail


def total_of(recv_ref):
    total = recv_ref[0, :PROBES, :].astype(f32)
    for piece in range(1, GROUP):
        total = total + recv_ref[piece, :PROBES, :].astype(f32)
    return total


def send_all(send_ref, vector, tail):
    for dest in range(GROUP):
        send_ref[dest, :PROBES] = vector
        send_ref[dest, PROBES:] = tail


def after_first(recv_ref, direction_ref, image_ref, send_ref):
    product = total_of(recv_ref)
    direction = direction_ref[...]
    shifted = product + (noise_level - SHIFT_1) * direction
    image_ref[...] = product
    sums = as_rows([lane_sum(direction * shifted), lane_sum(shifted * shifted)])
    send_all(send_ref, shifted.astype(bf16), tail_rows(sums))


def after_second(recv_ref, direction_ref, image_ref, send_ref, known_ref):
    along, square = tail_sums((recv_ref,), 2)
    scale = BETA_1 * BETA_1
    alpha_1 = (along + SHIFT_1 * N) / scale
    excess = alpha_1 - SHIFT_1
    squares_2 = jnp.maximum(square - 2.0 * excess * along + excess * excess * N, 0.0) / scale
    beta_2 = jnp.sqrt(squares_2 + epsilon)
    known_ref[...] = stack_rows([alpha_1, beta_2], (8, PROBES))
    excess, over, beta = as_columns([excess, 1.0 / beta_2, beta_2 * (1.0 / BETA_1)])
    product = total_of(recv_ref)
    direction, image = direction_ref[...], image_ref[...]
    shifted = image + (noise_level - SHIFT_1) * direction
    second = (shifted - excess * direction) * (1.0 / BETA_1)
    moved = (product - excess * image) * (1.0 / BETA_1)
    third = (moved + (noise_level - SHIFT_2) * second) * over - beta * direction
    sums = as_rows(
        [
            lane_sum(second * moved),
            lane_sum(third * third),
            lane_sum(third * second),
            lane_sum(third * moved),
            lane_sum(second * second),
        ]
    )
    send_all(send_ref, third.astype(bf16), tail_rows(sums))


def multiply_third(
    kernel_ref, before_ref, mine_ref, recv_ref, own_ref, out_ref, send_ref
):
    out_ref[...] = before_ref[...] + multiply(kernel_ref, recv_ref)
    send_all(send_ref, own_ref[0, :PROBES, :], tail_rows(tail_sums((mine_ref, recv_ref), 5)))


def quadratic(product_ref, right_ref, out_ref, sums_ref):
    (quad,) = as_rows([lane_sum(wide(right_ref).astype(f32) * product_ref[...])])
    out_ref[...] = jnp.broadcast_to(quad[None], out_ref.shape)
    sums_ref[...] = stack_rows(tail_sums((right_ref,), 5), (8, PROBES))


def log_weight(alpha_list, beta_list):
    degree = len(alpha_list)
    zeros_row = jnp.zeros(alpha_list[0].shape, f32)
    ones_row = jnp.ones(alpha_list[0].shape, f32)
    matrix = [[zeros_row] * degree for _ in range(degree)]
    vectors = [[zeros_row] * degree for _ in range(degree)]
    for idx in range(degree):
        matrix[idx][idx] = alpha_list[idx]
        vectors[idx][idx] = ones_row
        if idx + 1 < degree:
            matrix[idx][idx + 1] = beta_list[idx]
            matrix[idx + 1][idx] = beta_list[idx]
    for _ in range(jacobi_sweeps):
        for p in range(degree):
            for q in range(p + 1, degree):
                rotate_by = 0.5 * jnp.arctan2(2.0 * matrix[p][q], matrix[q][q] - matrix[p][p])
                cosine = jnp.cos(rotate_by)
                sine = jnp.sin(rotate_by)
                for grid in (matrix, vectors):
                    for row in grid:
                        left, right = row[p], row[q]
                        row[p] = cosine * left - sine * right
                        row[q] = sine * left + cosine * right
                for col in range(degree):
                    upper, lower = matrix[p][col], matrix[q][col]
                    matrix[p][col] = cosine * upper - sine * lower
                    matrix[q][col] = sine * upper + cosine * lower
    total = zeros_row
    for k in range(degree):
        total = total + vectors[0][k] * vectors[0][k] * jnp.log(matrix[k][k])
    return total


def swap_cores(value):
    return lax.ppermute(value, "core", [(0, 1), (1, 0)])


def exchange(value, axes):
    return lax.all_to_all(value, axes, 0, 0, tiled=True)


def per_device(points, inverse_scales, probe_signs):
    piece = resident((PROBES, PIECE), f32)
    padded = resident((GROUP, PROBES + TAIL, PIECE), bf16)
    block = resident((PROBES, BLOCK), f32)
    kernel_half = resident((BLOCK, BLOCK), bf16)
    scratch = [pltpu.VMEM((BLOCK, FEATURES), bf16), pltpu.VMEM((FEATURES, BLOCK), bf16)]
    send, right, direction = call(
        prepare,
        (
            resident((GROUP, PROBES + 64, PIECE), bf16),
            resident((GROUP, 64, PIECE), bf16),
            piece,
        ),
        points,
        inverse_scales[None],
        probe_signs,
        in_specs=[pl.BlockSpec(memory_space=pl.ANY)] * 3,
        limit=58,
        scratch=[
            pltpu.VMEM((DIM, PIECE), f32),
            pltpu.VMEM((1, DIM), f32),
            pltpu.VMEM((PIECE, PROBES), jnp.int32),
            pltpu.SemaphoreType.DMA((3,)),
        ],
    )
    mine = exchange(send, COL)
    other = swap_cores(mine)
    right = exchange(right, ROW)
    kernel_mine, total = call(evaluate_first, (kernel_half, block), mine, right, scratch=scratch)
    kernel_other, total = call(
        evaluate_second,
        (kernel_half, resident((GROUP, PROBES, PIECE), bf16)),
        other,
        right,
        total,
        scratch=scratch,
    )
    recv = exchange(total, ROW)
    image, send = call(after_first, (piece, padded), recv, direction)
    mine = exchange(send, COL)
    other = swap_cores(mine)
    (total,) = call(multiply_first, (block,), kernel_mine, mine)
    (send,) = call(multiply_second, (padded,), kernel_other, total, mine, other)
    recv = exchange(send, ROW)
    own, known = call(
        after_second, (padded, resident((8, PROBES), f32)), recv, direction, image
    )
    mine = exchange(own, COL)
    other = swap_cores(mine)
    (total,) = call(multiply_first, (block,), kernel_mine, mine)
    total, send = call(
        multiply_third, (block, padded), kernel_other, total, mine, other, own
    )
    right = exchange(send, ROW)
    quad, sums = call(
        quadratic,
        (resident((128, 1, PROBES), f32), resident((8, PROBES), f32)),
        total,
        right,
    )
    quad = jnp.sum(exchange(quad, AXES), axis=(0, 1))
    alpha_1, beta_2 = known[0], known[1]
    scale = beta_2 * beta_2
    alpha_2 = (sums[0] + noise_level * sums[4]) / scale
    turn = (alpha_2 - SHIFT_2) / beta_2
    squares_3 = jnp.maximum(sums[1] - 2.0 * turn * sums[2] + turn * turn * sums[4], 0.0)
    curvature_3 = quad - 2.0 * turn * sums[3] + turn * turn * sums[0] + noise_level * squares_3
    beta_3 = jnp.sqrt(squares_3 + epsilon)
    alpha_3 = curvature_3 / (beta_3 * beta_3)
    return alpha_1, log_weight([alpha_1, alpha_2, alpha_3], [beta_2, beta_3])


def solution(mesh):
    split = Mesh(mesh.devices.reshape(2, 4, 2, 4, 2), AXES)
    return jax.shard_map(
        per_device,
        mesh=split,
        in_specs=(P(None, AXES), P(), P(AXES, None)),
        out_specs=(P(), P()),
        check_vma=False,
    )
```

```python
import math

import jax
import jax.numpy as jnp
from jax import lax
from jax.experimental import pallas as pl
from jax.experimental.pallas import tpu as pltpu
from jax.sharding import Mesh
from jax.sharding import PartitionSpec as P

AXES = ("x_lo", "z", "x_hi", "y", "core")
ROW = ("x_lo", "z")
COL = ("x_hi", "y")

N = 32768
DIM = 16
PIECE = 256
PROBES = 128
GROUP = 8
BLOCK = GROUP * PIECE
FEATURES = 128
TAIL = 16

epsilon = 1e-06
noise_level = 1.0
jacobi_sweeps = 6

BETA_1 = math.sqrt(N + epsilon)
SHIFT_1 = 2.0

bf16 = jnp.bfloat16
f32 = jnp.float32


def resident(shape, dtype):
    return pltpu.VMEM(shape, dtype)


def call(body, outs, *args, scratch=(), in_specs=None, limit=12):
    whole = pl.BlockSpec(memory_space=pltpu.VMEM)
    return pl.pallas_call(
        body,
        out_shape=tuple(outs),
        in_specs=in_specs or [whole] * len(args),
        out_specs=tuple([whole] * len(outs)),
        scratch_shapes=list(scratch),
        compiler_params=pltpu.CompilerParams(vmem_limit_bytes=limit * 2**20),
    )(*args)


def parts(value):
    high = value.astype(bf16)
    rest = value - high.astype(f32)
    middle = rest.astype(bf16)
    low = (rest - middle.astype(f32)).astype(bf16)
    return high, middle, low


def stack_rows(values, shape):
    row = lax.broadcasted_iota(jnp.int32, shape, 0)
    block = jnp.zeros(shape, f32)
    for place, value in enumerate(values):
        block = jnp.where(row == place, jnp.broadcast_to(value, shape), block)
    return block


def as_rows(columns):
    lane = lax.broadcasted_iota(jnp.int32, (PROBES, PROBES), 1)
    block = jnp.zeros((PROBES, PROBES), f32)
    for place, value in enumerate(columns):
        block = jnp.where(lane == place, value, block)
    block = block.T
    return [block[place : place + 1] for place in range(len(columns))]


def as_columns(rows):
    block = stack_rows(rows, (PROBES, PROBES)).T
    return [block[:, place : place + 1] for place in range(len(rows))]


def lane_sum(value):
    return jnp.sum(value, axis=1, keepdims=True)


def tail_rows(rows):
    values = [part.astype(f32) for row in rows for part in parts(row)]
    block = stack_rows(values, (TAIL, PROBES))
    return jnp.concatenate([block, jnp.zeros_like(block)], axis=1).astype(bf16)


def total_rows(total, count):
    return [
        total[3 * k : 3 * k + 1] + total[3 * k + 1 : 3 * k + 2] + total[3 * k + 2 : 3 * k + 3]
        for k in range(count)
    ]


def tail_sums(refs, count):
    total = jnp.zeros((TAIL, PROBES), f32)
    for ref in refs:
        for piece in range(GROUP):
            total = total + ref[piece, PROBES:, :PROBES].astype(f32)
    return total_rows(total, count)


def prepare(
    points_hbm,
    scales_hbm,
    signs_hbm,
    send_ref,
    right_ref,
    direction_ref,
    points_ref,
    scales_ref,
    signs_ref,
    sems,
):
    copies = [
        pltpu.make_async_copy(src, dst, sems.at[i])
        for i, (src, dst) in enumerate(
            ((points_hbm, points_ref), (scales_hbm, scales_ref), (signs_hbm, signs_ref))
        )
    ]
    for copy in copies:
        copy.start()
    for copy in copies:
        copy.wait()
    square = (DIM, DIM)
    same = lax.broadcasted_iota(jnp.int32, square, 0) == lax.broadcasted_iota(jnp.int32, square, 1)
    scales = lane_sum(jnp.where(same, jnp.broadcast_to(scales_ref[...], square), 0.0))
    scaled = points_ref[...] * scales * math.sqrt(math.log2(math.e))
    norms = -0.5 * jnp.sum(scaled * scaled, axis=0, keepdims=True)
    pieces = [part.astype(f32) for part in parts(norms)]
    one = jnp.ones((1, PIECE), f32)
    shape = (16, PIECE)
    points = list(parts(scaled))
    left = jnp.concatenate(points + [stack_rows(pieces + [one] * 3, shape).astype(bf16)], axis=0)
    right = jnp.concatenate(points + [stack_rows([one] * 3 + pieces, shape).astype(bf16)], axis=0)
    direction = (2.0 * signs_ref[...].astype(f32) - 1.0).T
    direction_ref[...] = direction
    half = direction.astype(bf16)
    for dest in range(GROUP):
        send_ref[dest, :PROBES] = half
        send_ref[dest, PROBES:] = left
        right_ref[dest] = right


def features(read, order):
    rows = [read(16 * part) for part in order]
    return jnp.concatenate(rows + [jnp.zeros((16, PIECE), bf16)], axis=0)


def wide(ref):
    return jnp.concatenate([ref[piece, :PROBES, :] for piece in range(GROUP)], axis=1)


def span(piece):
    return slice(piece * PIECE, (piece + 1) * PIECE)


def evaluate(recv_ref, right_ref, kernel_ref, left, right):
    for piece in range(GROUP):
        left[span(piece), :] = features(
            lambda b: recv_ref[piece, PROBES + b : PROBES + b + 16, :], (0, 0, 1, 0, 2, 1, 3)
        ).T
        right[:, span(piece)] = features(
            lambda b: right_ref[piece, b : b + 16, :], (0, 1, 0, 2, 0, 1, 3)
        )

    def tile(step, carry):
        rows = pl.ds(pl.multiple_of(step * 512, 512), 512)
        for piece in range(GROUP):
            power = jnp.dot(left[rows, :], right[:, span(piece)], preferred_element_type=f32)
            kernel_ref[rows, span(piece)] = jnp.exp2(jnp.minimum(power, 0.0)).astype(bf16)
        return carry

    lax.fori_loop(0, BLOCK // 512, tile, 0)


def evaluate_first(recv_ref, right_ref, kernel_ref, out_ref, left, right):
    evaluate(recv_ref, right_ref, kernel_ref, left, right)
    out_ref[...] = multiply(kernel_ref, recv_ref)


def evaluate_second(recv_ref, right_ref, before_ref, kernel_ref, partial_ref, out_ref, left, right):
    evaluate(recv_ref, right_ref, kernel_ref, left, right)
    total = before_ref[...] + multiply(kernel_ref, recv_ref)
    partial_ref[...] = total
    for piece in range(GROUP):
        out_ref[piece] = total[:, span(piece)].astype(bf16)


def multiply(kernel_ref, recv_ref):
    return jnp.dot(wide(recv_ref), kernel_ref[...], preferred_element_type=f32)


def multiply_first(kernel_ref, recv_ref, out_ref):
    out_ref[...] = multiply(kernel_ref, recv_ref)


def multiply_second(kernel_ref, before_ref, mine_ref, recv_ref, partial_ref, out_ref):
    total = before_ref[...] + multiply(kernel_ref, recv_ref)
    partial_ref[...] = total
    tail = tail_rows(tail_sums((mine_ref, recv_ref), 2))
    for piece in range(GROUP):
        out_ref[piece, :PROBES] = total[:, span(piece)].astype(bf16)
        out_ref[piece, PROBES:] = tail


def total_of(recv_ref):
    total = recv_ref[0, :PROBES, :].astype(f32)
    for piece in range(1, GROUP):
        total = total + recv_ref[piece, :PROBES, :].astype(f32)
    return total


def send_all(send_ref, vector, tail):
    for dest in range(GROUP):
        send_ref[dest, :PROBES] = vector
        send_ref[dest, PROBES:] = tail


def after_first(recv_ref, direction_ref, image_ref, send_ref):
    product = total_of(recv_ref)
    direction = direction_ref[...]
    shifted = product + (noise_level - SHIFT_1) * direction
    image_ref[...] = product
    sums = as_rows([lane_sum(direction * shifted), lane_sum(shifted * shifted)])
    send_all(send_ref, shifted.astype(bf16), tail_rows(sums))


def after_second(
    recv_ref, direction_ref, image_ref, send_ref, pair_ref, known_ref, third_ref, second_ref
):
    along, square = tail_sums((recv_ref,), 2)
    scale = BETA_1 * BETA_1
    alpha_1 = (along + SHIFT_1 * N) / scale
    excess = alpha_1 - SHIFT_1
    squares_2 = jnp.maximum(square - 2.0 * excess * along + excess * excess * N, 0.0) / scale
    beta_2 = jnp.sqrt(squares_2 + epsilon)
    known_ref[...] = stack_rows([alpha_1, beta_2], (8, PROBES))
    excess, over, beta = as_columns([excess, 1.0 / beta_2, beta_2 * (1.0 / BETA_1)])
    product = total_of(recv_ref)
    direction, image = direction_ref[...], image_ref[...]
    shifted = image + (noise_level - SHIFT_1) * direction
    second = (shifted - excess * direction) * (1.0 / BETA_1)
    moved = (product - excess * image) * (1.0 / BETA_1)
    third = moved * over - beta * direction
    second_ref[...] = second
    third_ref[...] = third
    sums = as_rows([lane_sum(second * moved), lane_sum(second * second)])
    half = third.astype(bf16)
    send_all(send_ref, half, tail_rows(sums))
    pair_ref[:PROBES] = half
    pair_ref[PROBES:] = second.astype(bf16)


def multiply_third(kernel_ref, before_ref, mine_ref, recv_ref, pair_ref, out_ref, send_ref):
    out_ref[...] = before_ref[...] + multiply(kernel_ref, recv_ref)
    tail = tail_rows(tail_sums((mine_ref, recv_ref), 2))
    for dest in range(GROUP):
        send_ref[dest, : 2 * PROBES] = pair_ref[...]
        send_ref[dest, 2 * PROBES :] = tail


def quadratic(
    product_ref,
    first_ref,
    second_ref,
    right_ref,
    known_ref,
    own_third_ref,
    own_second_ref,
    out_ref,
    known_out_ref,
):
    total = jnp.zeros((TAIL, PROBES), f32)
    for piece in range(GROUP):
        total = total + right_ref[piece, 2 * PROBES :, :PROBES].astype(f32)
    along, squares_2 = total_rows(total, 2)
    alpha_1, beta_2 = known_ref[0:1], known_ref[1:2]
    alpha_2 = (along + noise_level * squares_2) / (beta_2 * beta_2)
    known_out_ref[...] = stack_rows([alpha_1, beta_2, alpha_2], (8, PROBES))
    turn = (alpha_2 - noise_level) / beta_2
    turn, excess = as_columns([turn, alpha_1 - SHIFT_1])
    slope = turn * (1.0 / BETA_1)
    quad = jnp.zeros((PROBES, 1), f32)
    for piece in range(GROUP):
        cut = span(piece)
        moved = product_ref[:, cut] - slope * (second_ref[:, cut] - excess * first_ref[:, cut])
        third = right_ref[piece, :PROBES, :].astype(f32) - turn * right_ref[
            piece, PROBES : 2 * PROBES, :
        ].astype(f32)
        quad = quad + lane_sum(third * moved)
    own = own_third_ref[...] - turn * own_second_ref[...]
    rows = jnp.concatenate(as_rows([quad, lane_sum(own * own)]), axis=1)
    out_ref[...] = jnp.broadcast_to(rows[None], out_ref.shape)


def finish(recv_ref, known_ref, trace_ref, logdet_ref):
    sums = jnp.sum(recv_ref[...], axis=0)
    quad, squares_3 = sums[:, :PROBES], sums[:, PROBES:]
    alpha_1, beta_2, alpha_2 = known_ref[0:1], known_ref[1:2], known_ref[2:3]
    beta_3 = jnp.sqrt(squares_3 + epsilon)
    alpha_3 = (quad + noise_level * squares_3) / (beta_3 * beta_3)
    trace_ref[...] = alpha_1
    logdet_ref[...] = log_weight([alpha_1, alpha_2, alpha_3], [beta_2, beta_3])


def rotation(coupling, difference):
    square = coupling * coupling + difference * difference
    flat = square == 0.0
    inverse = lax.rsqrt(jnp.where(flat, 1.0, square))
    upper = 0.5 + 0.5 * jnp.abs(difference) * inverse
    root = lax.rsqrt(upper)
    large = upper * root
    small = 0.5 * jnp.abs(coupling) * inverse * root
    ahead = difference >= 0.0
    cosine = jnp.where(ahead, large, small)
    sine = jnp.where(ahead, small, large)
    sine = jnp.where(coupling < 0.0, -sine, sine)
    return jnp.where(flat, 1.0, cosine), jnp.where(flat, 0.0, sine)


def log_weight(alpha_list, beta_list):
    zero = jnp.zeros_like(alpha_list[0])
    entry = {(k, k): alpha_list[k] for k in range(3)}
    entry[0, 1], entry[1, 2], entry[0, 2] = beta_list[0], beta_list[1], zero
    first = [zero + 1.0, zero, zero]
    for _ in range(jacobi_sweeps):
        for p, q in ((0, 1), (0, 2), (1, 2)):
            k = 3 - p - q
            pk, qk = (min(p, k), max(p, k)), (min(q, k), max(q, k))
            a, b, d = entry[p, p], entry[p, q], entry[q, q]
            c, s = rotation(2.0 * b, d - a)
            cc, ss, cs = c * c, s * s, c * s
            entry[p, p] = cc * a - 2.0 * cs * b + ss * d
            entry[q, q] = ss * a + 2.0 * cs * b + cc * d
            entry[p, q] = (cc - ss) * b + cs * (a - d)
            entry[pk], entry[qk] = c * entry[pk] - s * entry[qk], s * entry[pk] + c * entry[qk]
            first[p], first[q] = c * first[p] - s * first[q], s * first[p] + c * first[q]
    total = zero
    for k in range(3):
        total = total + first[k] * first[k] * jnp.log(entry[k, k])
    return total


def swap_cores(value):
    return lax.ppermute(value, "core", [(0, 1), (1, 0)])


def exchange(value, axes):
    return lax.all_to_all(value, axes, 0, 0, tiled=True)


def per_device(points, inverse_scales, probe_signs):
    piece = resident((PROBES, PIECE), f32)
    padded = resident((GROUP, PROBES + TAIL, PIECE), bf16)
    block = resident((PROBES, BLOCK), f32)
    kernel_half = resident((BLOCK, BLOCK), bf16)
    scratch = [pltpu.VMEM((BLOCK, FEATURES), bf16), pltpu.VMEM((FEATURES, BLOCK), bf16)]
    send, right, direction = call(
        prepare,
        (
            resident((GROUP, PROBES + 64, PIECE), bf16),
            resident((GROUP, 64, PIECE), bf16),
            piece,
        ),
        points,
        inverse_scales[None],
        probe_signs,
        in_specs=[pl.BlockSpec(memory_space=pl.ANY)] * 3,
        limit=58,
        scratch=[
            pltpu.VMEM((DIM, PIECE), f32),
            pltpu.VMEM((1, DIM), f32),
            pltpu.VMEM((PIECE, PROBES), jnp.int32),
            pltpu.SemaphoreType.DMA((3,)),
        ],
    )
    mine = exchange(send, COL)
    other = swap_cores(mine)
    right = exchange(right, ROW)
    kernel_mine, total = call(evaluate_first, (kernel_half, block), mine, right, scratch=scratch)
    kernel_other, partial_1, total = call(
        evaluate_second,
        (kernel_half, block, resident((GROUP, PROBES, PIECE), bf16)),
        other,
        right,
        total,
        scratch=scratch,
    )
    recv = exchange(total, ROW)
    image, send = call(after_first, (piece, padded), recv, direction)
    mine = exchange(send, COL)
    other = swap_cores(mine)
    (total,) = call(multiply_first, (block,), kernel_mine, mine)
    partial_2, send = call(multiply_second, (block, padded), kernel_other, total, mine, other)
    recv = exchange(send, ROW)
    own, pair, known, third, second = call(
        after_second,
        (
            padded,
            resident((2 * PROBES, PIECE), bf16),
            resident((8, PROBES), f32),
            piece,
            piece,
        ),
        recv,
        direction,
        image,
    )
    mine = exchange(own, COL)
    other = swap_cores(mine)
    (total,) = call(multiply_first, (block,), kernel_mine, mine)
    total, send = call(
        multiply_third,
        (block, resident((GROUP, 2 * PROBES + TAIL, PIECE), bf16)),
        kernel_other,
        total,
        mine,
        other,
        pair,
    )
    right = exchange(send, ROW)
    sums, known = call(
        quadratic,
        (resident((128, 1, 2 * PROBES), f32), resident((8, PROBES), f32)),
        total,
        partial_1,
        partial_2,
        right,
        known,
        third,
        second,
    )
    row = jax.ShapeDtypeStruct((1, PROBES), f32)
    trace, logdet = call(finish, (row, row), exchange(sums, AXES), known)
    return trace[0], logdet[0]


def solution(mesh):
    split = Mesh(mesh.devices.reshape(2, 4, 2, 4, 2), AXES)
    return jax.shard_map(
        per_device,
        mesh=split,
        in_specs=(P(None, AXES), P(), P(AXES, None)),
        out_specs=(P(), P()),
        check_vma=False,
    )
```

```python
import math

import jax
import jax.numpy as jnp
from jax import lax
from jax.experimental import pallas as pl
from jax.experimental.pallas import tpu as pltpu
from jax.sharding import Mesh
from jax.sharding import PartitionSpec as P

AXES = ("x_lo", "z", "x_hi", "y", "core")
ROW = ("x_lo", "z")
COL = ("x_hi", "y")

N = 32768
DIM = 16
PIECE = 256
PROBES = 128
GROUP = 8
BLOCK = GROUP * PIECE
FEATURES = 128
TAIL = 16

epsilon = 1e-06
noise_level = 1.0
jacobi_sweeps = 6

BETA_1 = math.sqrt(N + epsilon)
SHIFT_1 = 2.0

bf16 = jnp.bfloat16
f32 = jnp.float32


def resident(shape, dtype):
    return pltpu.VMEM(shape, dtype)


def call(body, outs, *args, scratch=(), in_specs=None, limit=12):
    whole = pl.BlockSpec(memory_space=pltpu.VMEM)
    return pl.pallas_call(
        body,
        out_shape=tuple(outs),
        in_specs=in_specs or [whole] * len(args),
        out_specs=tuple([whole] * len(outs)),
        scratch_shapes=list(scratch),
        compiler_params=pltpu.CompilerParams(vmem_limit_bytes=limit * 2**20),
    )(*args)


def parts(value):
    high = value.astype(bf16)
    rest = value - high.astype(f32)
    middle = rest.astype(bf16)
    low = (rest - middle.astype(f32)).astype(bf16)
    return high, middle, low


def stack_rows(values, shape):
    row = lax.broadcasted_iota(jnp.int32, shape, 0)
    block = jnp.zeros(shape, f32)
    for place, value in enumerate(values):
        block = jnp.where(row == place, jnp.broadcast_to(value, shape), block)
    return block


def as_rows(columns):
    lane = lax.broadcasted_iota(jnp.int32, (PROBES, PROBES), 1)
    block = jnp.zeros((PROBES, PROBES), f32)
    for place, value in enumerate(columns):
        block = jnp.where(lane == place, value, block)
    block = block.T
    return [block[place : place + 1] for place in range(len(columns))]


def as_columns(rows):
    block = stack_rows(rows, (PROBES, PROBES)).T
    return [block[:, place : place + 1] for place in range(len(rows))]


def lane_sum(value):
    return jnp.sum(value, axis=1, keepdims=True)


def tail_rows(rows):
    values = [part.astype(f32) for row in rows for part in parts(row)]
    block = stack_rows(values, (TAIL, PROBES))
    return jnp.concatenate([block, jnp.zeros_like(block)], axis=1).astype(bf16)


def total_rows(total, count):
    return [
        total[3 * k : 3 * k + 1] + total[3 * k + 1 : 3 * k + 2] + total[3 * k + 2 : 3 * k + 3]
        for k in range(count)
    ]


def tail_sums(refs, count):
    total = jnp.zeros((TAIL, PROBES), f32)
    for ref in refs:
        for piece in range(GROUP):
            total = total + ref[piece, PROBES:, :PROBES].astype(f32)
    return total_rows(total, count)


def prepare(
    points_hbm,
    scales_hbm,
    signs_hbm,
    send_ref,
    right_ref,
    direction_ref,
    points_ref,
    scales_ref,
    signs_ref,
    sems,
):
    copies = [
        pltpu.make_async_copy(src, dst, sems.at[i])
        for i, (src, dst) in enumerate(
            ((points_hbm, points_ref), (scales_hbm, scales_ref), (signs_hbm, signs_ref))
        )
    ]
    for copy in copies:
        copy.start()
    for copy in copies:
        copy.wait()
    square = (DIM, DIM)
    same = lax.broadcasted_iota(jnp.int32, square, 0) == lax.broadcasted_iota(jnp.int32, square, 1)
    scales = lane_sum(jnp.where(same, jnp.broadcast_to(scales_ref[...], square), 0.0))
    scaled = points_ref[...] * scales * math.sqrt(math.log2(math.e))
    norms = -0.5 * jnp.sum(scaled * scaled, axis=0, keepdims=True)
    pieces = [part.astype(f32) for part in parts(norms)]
    one = jnp.ones((1, PIECE), f32)
    shape = (16, PIECE)
    points = list(parts(scaled))
    left = jnp.concatenate(points + [stack_rows(pieces + [one] * 3, shape).astype(bf16)], axis=0)
    right = jnp.concatenate(points + [stack_rows([one] * 3 + pieces, shape).astype(bf16)], axis=0)
    direction = (2.0 * signs_ref[...].astype(f32) - 1.0).T
    direction_ref[...] = direction
    half = direction.astype(bf16)
    for dest in range(GROUP):
        send_ref[dest, :PROBES] = half
        send_ref[dest, PROBES:] = left
        right_ref[dest] = right


def features(read, order):
    rows = [read(16 * part) for part in order]
    return jnp.concatenate(rows + [jnp.zeros((16, PIECE), bf16)], axis=0)


def wide(ref):
    return jnp.concatenate([ref[piece, :PROBES, :] for piece in range(GROUP)], axis=1)


def span(piece):
    return slice(piece * PIECE, (piece + 1) * PIECE)


def evaluate(recv_ref, kernel_ref, left, right):
    for piece in range(GROUP):
        left[span(piece), :] = features(
            lambda b: recv_ref[piece, PROBES + b : PROBES + b + 16, :], (0, 0, 1, 0, 2, 1, 3)
        ).T
    tall = 1024

    def tile(step, carry):
        rows = pl.ds(pl.multiple_of(step * tall, tall), tall)
        for piece in range(GROUP):
            power = jnp.dot(left[rows, :], right[:, span(piece)], preferred_element_type=f32)
            kernel_ref[rows, span(piece)] = jnp.exp2(jnp.minimum(power, 0.0)).astype(bf16)
        return carry

    lax.fori_loop(0, BLOCK // tall, tile, 0)


def evaluate_first(recv_ref, right_ref, kernel_ref, out_ref, right, left):
    for piece in range(GROUP):
        right[:, span(piece)] = features(
            lambda b: right_ref[piece, b : b + 16, :], (0, 1, 0, 2, 0, 1, 3)
        )
    evaluate(recv_ref, kernel_ref, left, right)
    out_ref[...] = multiply(kernel_ref, recv_ref)


def evaluate_second(recv_ref, right, before_ref, kernel_ref, partial_ref, out_ref, left):
    evaluate(recv_ref, kernel_ref, left, right)
    total = before_ref[...] + multiply(kernel_ref, recv_ref)
    partial_ref[...] = total
    for piece in range(GROUP):
        out_ref[piece] = total[:, span(piece)].astype(bf16)


def multiply(kernel_ref, recv_ref):
    return jnp.dot(wide(recv_ref), kernel_ref[...], preferred_element_type=f32)


def multiply_first(kernel_ref, recv_ref, out_ref):
    out_ref[...] = multiply(kernel_ref, recv_ref)


def multiply_second(kernel_ref, before_ref, mine_ref, recv_ref, partial_ref, out_ref):
    total = before_ref[...] + multiply(kernel_ref, recv_ref)
    partial_ref[...] = total
    tail = tail_rows(tail_sums((mine_ref, recv_ref), 2))
    for piece in range(GROUP):
        out_ref[piece, :PROBES] = total[:, span(piece)].astype(bf16)
        out_ref[piece, PROBES:] = tail


def total_of(recv_ref):
    total = recv_ref[0, :PROBES, :].astype(f32)
    for piece in range(1, GROUP):
        total = total + recv_ref[piece, :PROBES, :].astype(f32)
    return total


def send_all(send_ref, vector, tail):
    for dest in range(GROUP):
        send_ref[dest, :PROBES] = vector
        send_ref[dest, PROBES:] = tail


def after_first(recv_ref, direction_ref, image_ref, send_ref):
    product = total_of(recv_ref)
    direction = direction_ref[...]
    shifted = product + (noise_level - SHIFT_1) * direction
    image_ref[...] = product
    sums = as_rows([lane_sum(direction * shifted), lane_sum(shifted * shifted)])
    send_all(send_ref, shifted.astype(bf16), tail_rows(sums))


def after_second(
    recv_ref, direction_ref, image_ref, pair_ref, known_ref, third_ref, second_ref
):
    along, square = tail_sums((recv_ref,), 2)
    scale = BETA_1 * BETA_1
    alpha_1 = (along + SHIFT_1 * N) / scale
    excess = alpha_1 - SHIFT_1
    squares_2 = jnp.maximum(square - 2.0 * excess * along + excess * excess * N, 0.0) / scale
    beta_2 = jnp.sqrt(squares_2 + epsilon)
    known_ref[...] = stack_rows([alpha_1, beta_2, squares_2], (8, PROBES))
    excess, over, beta = as_columns([excess, 1.0 / beta_2, beta_2 * (1.0 / BETA_1)])
    product = total_of(recv_ref)
    direction, image = direction_ref[...], image_ref[...]
    shifted = image + (noise_level - SHIFT_1) * direction
    second = (shifted - excess * direction) * (1.0 / BETA_1)
    moved = (product - excess * image) * (1.0 / BETA_1)
    third = (moved * over - beta * direction).astype(bf16)
    second_ref[...] = second
    third_ref[...] = third
    for dest in range(GROUP):
        pair_ref[dest, :PROBES] = third
        pair_ref[dest, PROBES:] = second.astype(bf16)


def pair_of(right_ref, piece):
    return right_ref[piece, :PROBES, :].astype(f32), right_ref[piece, PROBES:, :].astype(f32)


def join(right_ref, third_ref, send_ref):
    total = jnp.zeros((PROBES, PIECE), f32)
    for piece in range(GROUP):
        third, second = pair_of(right_ref, piece)
        total = total + third * second
    send_all(send_ref, third_ref[...], tail_rows(as_rows([lane_sum(total)])))


def multiply_third(
    kernel_ref,
    before_ref,
    mine_ref,
    recv_ref,
    first_ref,
    second_ref,
    right_ref,
    known_ref,
    own_third_ref,
    own_second_ref,
    out_ref,
    known_out_ref,
):
    (along,) = tail_sums((mine_ref, recv_ref), 1)
    alpha_1, beta_2, squares_2 = known_ref[0:1], known_ref[1:2], known_ref[2:3]
    scale = beta_2 * beta_2
    curvature = beta_2 * along + scale * alpha_1 * (epsilon / (BETA_1 * BETA_1))
    alpha_2 = (curvature + noise_level * squares_2) / scale
    known_out_ref[...] = stack_rows([alpha_1, beta_2, alpha_2], (8, PROBES))
    turn = (alpha_2 - noise_level) / beta_2
    turn, excess = as_columns([turn, alpha_1 - SHIFT_1])
    slope = turn * (1.0 / BETA_1)
    product = before_ref[...] + multiply(kernel_ref, recv_ref)
    total = jnp.zeros((PROBES, PIECE), f32)
    for piece in range(GROUP):
        cut = span(piece)
        moved = product[:, cut] - slope * (second_ref[:, cut] - excess * first_ref[:, cut])
        third, second = pair_of(right_ref, piece)
        total = total + (third - turn * second) * moved
    own = own_third_ref[...].astype(f32) - turn * own_second_ref[...]
    rows = jnp.concatenate(as_rows([lane_sum(total), lane_sum(own * own)]), axis=1)
    out_ref[...] = jnp.broadcast_to(rows[None], out_ref.shape)


def finish(recv_ref, known_ref, trace_ref, logdet_ref):
    sums = jnp.sum(recv_ref[...], axis=0)
    quad, squares_3 = sums[:, :PROBES], sums[:, PROBES:]
    alpha_1, beta_2, alpha_2 = known_ref[0:1], known_ref[1:2], known_ref[2:3]
    beta_3 = jnp.sqrt(squares_3 + epsilon)
    alpha_3 = (quad + noise_level * squares_3) / (beta_3 * beta_3)
    trace_ref[...] = alpha_1
    logdet_ref[...] = log_weight([alpha_1, alpha_2, alpha_3], [beta_2, beta_3])


def rotation(coupling, difference):
    square = coupling * coupling + difference * difference
    flat = square == 0.0
    inverse = lax.rsqrt(jnp.where(flat, 1.0, square))
    upper = 0.5 + 0.5 * jnp.abs(difference) * inverse
    root = lax.rsqrt(upper)
    large = upper * root
    small = 0.5 * jnp.abs(coupling) * inverse * root
    ahead = difference >= 0.0
    cosine = jnp.where(ahead, large, small)
    sine = jnp.where(ahead, small, large)
    sine = jnp.where(coupling < 0.0, -sine, sine)
    return jnp.where(flat, 1.0, cosine), jnp.where(flat, 0.0, sine)


def log_weight(alpha_list, beta_list):
    zero = jnp.zeros_like(alpha_list[0])
    entry = {(k, k): alpha_list[k] for k in range(3)}
    entry[0, 1], entry[1, 2], entry[0, 2] = beta_list[0], beta_list[1], zero
    first = [zero + 1.0, zero, zero]
    for _ in range(jacobi_sweeps):
        for p, q in ((0, 1), (0, 2), (1, 2)):
            k = 3 - p - q
            pk, qk = (min(p, k), max(p, k)), (min(q, k), max(q, k))
            a, b, d = entry[p, p], entry[p, q], entry[q, q]
            c, s = rotation(2.0 * b, d - a)
            cc, ss, cs = c * c, s * s, c * s
            entry[p, p] = cc * a - 2.0 * cs * b + ss * d
            entry[q, q] = ss * a + 2.0 * cs * b + cc * d
            entry[p, q] = (cc - ss) * b + cs * (a - d)
            entry[pk], entry[qk] = c * entry[pk] - s * entry[qk], s * entry[pk] + c * entry[qk]
            first[p], first[q] = c * first[p] - s * first[q], s * first[p] + c * first[q]
    total = zero
    for k in range(3):
        total = total + first[k] * first[k] * jnp.log(entry[k, k])
    return total


def swap_cores(value):
    return lax.ppermute(value, "core", [(0, 1), (1, 0)])


def exchange(value, axes):
    return lax.all_to_all(value, axes, 0, 0, tiled=True)


def per_device(points, inverse_scales, probe_signs):
    piece = resident((PROBES, PIECE), f32)
    padded = resident((GROUP, PROBES + TAIL, PIECE), bf16)
    block = resident((PROBES, BLOCK), f32)
    kernel_half = resident((BLOCK, BLOCK), bf16)
    scratch = [pltpu.VMEM((BLOCK, FEATURES), bf16)]
    send, right, direction = call(
        prepare,
        (
            resident((GROUP, PROBES + 64, PIECE), bf16),
            resident((GROUP, 64, PIECE), bf16),
            piece,
        ),
        points,
        inverse_scales[None],
        probe_signs,
        in_specs=[pl.BlockSpec(memory_space=pl.ANY)] * 3,
        limit=58,
        scratch=[
            pltpu.VMEM((DIM, PIECE), f32),
            pltpu.VMEM((1, DIM), f32),
            pltpu.VMEM((PIECE, PROBES), jnp.int32),
            pltpu.SemaphoreType.DMA((3,)),
        ],
    )
    mine = exchange(send, COL)
    other = swap_cores(mine)
    right = exchange(right, ROW)
    kernel_mine, total, right = call(
        evaluate_first,
        (kernel_half, block, resident((FEATURES, BLOCK), bf16)),
        mine,
        right,
        scratch=scratch,
    )
    kernel_other, partial_1, total = call(
        evaluate_second,
        (kernel_half, block, resident((GROUP, PROBES, PIECE), bf16)),
        other,
        right,
        total,
        scratch=scratch,
    )
    recv = exchange(total, ROW)
    image, send = call(after_first, (piece, padded), recv, direction)
    mine = exchange(send, COL)
    other = swap_cores(mine)
    (total,) = call(multiply_first, (block,), kernel_mine, mine)
    partial_2, send = call(multiply_second, (block, padded), kernel_other, total, mine, other)
    recv = exchange(send, ROW)
    pair, known, third, second = call(
        after_second,
        (
            resident((GROUP, 2 * PROBES, PIECE), bf16),
            resident((8, PROBES), f32),
            resident((PROBES, PIECE), bf16),
            piece,
        ),
        recv,
        direction,
        image,
    )
    right = exchange(pair, ROW)
    (send,) = call(join, (padded,), right, third)
    mine = exchange(send, COL)
    other = swap_cores(mine)
    (total,) = call(multiply_first, (block,), kernel_mine, mine)
    sums, known = call(
        multiply_third,
        (resident((128, 1, 2 * PROBES), f32), resident((8, PROBES), f32)),
        kernel_other,
        total,
        mine,
        other,
        partial_1,
        partial_2,
        right,
        known,
        third,
        second,
    )
    row = jax.ShapeDtypeStruct((1, PROBES), f32)
    trace, logdet = call(finish, (row, row), exchange(sums, AXES), known)
    return trace[0], logdet[0]


def solution(mesh):
    split = Mesh(mesh.devices.reshape(2, 4, 2, 4, 2), AXES)
    return jax.shard_map(
        per_device,
        mesh=split,
        in_specs=(P(None, AXES), P(), P(AXES, None)),
        out_specs=(P(), P()),
        check_vma=False,
    )
```

```python
import math

import jax
import jax.numpy as jnp
from jax import lax
from jax.experimental import pallas as pl
from jax.experimental.pallas import tpu as pltpu
from jax.sharding import Mesh
from jax.sharding import PartitionSpec as P

AXES = ("x_lo", "z", "x_hi", "y", "core")
ROW = ("x_lo", "z")
COL = ("x_hi", "y")

N = 32768
DIM = 16
PIECE = 256
PROBES = 128
GROUP = 8
BLOCK = GROUP * PIECE
FEATURES = 128
TAIL = 16

epsilon = 1e-06
noise_level = 1.0
jacobi_sweeps = 6

BETA_1 = math.sqrt(N + epsilon)
SHIFT_1 = 2.0

bf16 = jnp.bfloat16
f32 = jnp.float32


def resident(shape, dtype):
    return pltpu.VMEM(shape, dtype)


def call(body, outs, *args, scratch=(), in_specs=None, limit=12):
    whole = pl.BlockSpec(memory_space=pltpu.VMEM)
    return pl.pallas_call(
        body,
        out_shape=tuple(outs),
        in_specs=in_specs or [whole] * len(args),
        out_specs=tuple([whole] * len(outs)),
        scratch_shapes=list(scratch),
        compiler_params=pltpu.CompilerParams(vmem_limit_bytes=limit * 2**20),
    )(*args)


def parts(value):
    high = value.astype(bf16)
    rest = value - high.astype(f32)
    middle = rest.astype(bf16)
    low = (rest - middle.astype(f32)).astype(bf16)
    return high, middle, low


def stack_rows(values, shape):
    row = lax.broadcasted_iota(jnp.int32, shape, 0)
    block = jnp.zeros(shape, f32)
    for place, value in enumerate(values):
        block = jnp.where(row == place, jnp.broadcast_to(value, shape), block)
    return block


def as_rows(columns):
    lane = lax.broadcasted_iota(jnp.int32, (PROBES, PROBES), 1)
    block = jnp.zeros((PROBES, PROBES), f32)
    for place, value in enumerate(columns):
        block = jnp.where(lane == place, value, block)
    block = block.T
    return [block[place : place + 1] for place in range(len(columns))]


def as_columns(rows):
    block = stack_rows(rows, (PROBES, PROBES)).T
    return [block[:, place : place + 1] for place in range(len(rows))]


def lane_sum(value):
    return jnp.sum(value, axis=1, keepdims=True)


def tail_rows(rows):
    values = [part.astype(f32) for row in rows for part in parts(row)]
    block = stack_rows(values, (TAIL, PROBES))
    return jnp.concatenate([block, jnp.zeros_like(block)], axis=1).astype(bf16)


def total_rows(total, count):
    return [
        total[3 * k : 3 * k + 1] + total[3 * k + 1 : 3 * k + 2] + total[3 * k + 2 : 3 * k + 3]
        for k in range(count)
    ]


def tail_sums(refs, count):
    total = jnp.zeros((TAIL, PROBES), f32)
    for ref in refs:
        for piece in range(GROUP):
            total = total + ref[piece, PROBES:, :PROBES].astype(f32)
    return total_rows(total, count)


def prepare(
    points_hbm,
    scales_hbm,
    signs_hbm,
    send_ref,
    right_ref,
    direction_ref,
    points_ref,
    scales_ref,
    signs_ref,
    sems,
):
    copies = [
        pltpu.make_async_copy(src, dst, sems.at[i])
        for i, (src, dst) in enumerate(
            ((points_hbm, points_ref), (scales_hbm, scales_ref), (signs_hbm, signs_ref))
        )
    ]
    for copy in copies:
        copy.start()
    for copy in copies:
        copy.wait()
    square = (DIM, DIM)
    same = lax.broadcasted_iota(jnp.int32, square, 0) == lax.broadcasted_iota(jnp.int32, square, 1)
    scales = lane_sum(jnp.where(same, jnp.broadcast_to(scales_ref[...], square), 0.0))
    scaled = points_ref[...] * scales * math.sqrt(math.log2(math.e))
    norms = -0.5 * jnp.sum(scaled * scaled, axis=0, keepdims=True)
    pieces = [part.astype(f32) for part in parts(norms)]
    one = jnp.ones((1, PIECE), f32)
    shape = (16, PIECE)
    points = list(parts(scaled))
    left = jnp.concatenate(points + [stack_rows(pieces + [one] * 3, shape).astype(bf16)], axis=0)
    right = jnp.concatenate(points + [stack_rows([one] * 3 + pieces, shape).astype(bf16)], axis=0)
    direction = (2.0 * signs_ref[...].astype(f32) - 1.0).T
    direction_ref[...] = direction
    half = direction.astype(bf16)
    for dest in range(GROUP):
        send_ref[dest, :PROBES] = half
        send_ref[dest, PROBES:] = left
        right_ref[dest] = right


def features(read, order):
    rows = [read(16 * part) for part in order]
    return jnp.concatenate(rows + [jnp.zeros((16, PIECE), bf16)], axis=0)


def wide(ref):
    return jnp.concatenate([ref[piece, :PROBES, :] for piece in range(GROUP)], axis=1)


def span(piece):
    return slice(piece * PIECE, (piece + 1) * PIECE)


def evaluate(mine_ref, other_ref, right_ref, kernel_ref, partial_ref, out_ref, left, right):
    for piece in range(GROUP):
        right[:, span(piece)] = features(
            lambda b: right_ref[piece, b : b + 16, :], (0, 1, 0, 2, 0, 1, 3)
        )
        for half, recv_ref in enumerate((mine_ref, other_ref)):
            left[span(half * GROUP + piece), :] = features(
                lambda b: recv_ref[piece, PROBES + b : PROBES + b + 16, :], (0, 0, 1, 0, 2, 1, 3)
            ).T
    tall = 1024

    def tile(step, carry):
        rows = pl.ds(pl.multiple_of(step * tall, tall), tall)
        for piece in range(GROUP):
            power = jnp.dot(left[rows, :], right[:, span(piece)], preferred_element_type=f32)
            kernel_ref[rows, span(piece)] = jnp.exp2(jnp.minimum(power, 0.0)).astype(bf16)
        return carry

    lax.fori_loop(0, 2 * BLOCK // tall, tile, 0)
    vectors = jnp.concatenate([wide(mine_ref), wide(other_ref)], axis=1)
    total = jnp.dot(vectors, kernel_ref[...], preferred_element_type=f32)
    partial_ref[...] = total
    for piece in range(GROUP):
        out_ref[piece] = total[:, span(piece)].astype(bf16)


def multiply(kernel_ref, recv_ref, half):
    rows = slice(half * BLOCK, (half + 1) * BLOCK)
    return jnp.dot(wide(recv_ref), kernel_ref[rows, :], preferred_element_type=f32)


def multiply_first(kernel_ref, recv_ref, out_ref):
    out_ref[...] = multiply(kernel_ref, recv_ref, 0)


def multiply_second(kernel_ref, before_ref, mine_ref, recv_ref, partial_ref, out_ref):
    total = before_ref[...] + multiply(kernel_ref, recv_ref, 1)
    partial_ref[...] = total
    tail = tail_rows(tail_sums((mine_ref, recv_ref), 2))
    for piece in range(GROUP):
        out_ref[piece, :PROBES] = total[:, span(piece)].astype(bf16)
        out_ref[piece, PROBES:] = tail


def total_of(recv_ref):
    total = recv_ref[0, :PROBES, :].astype(f32)
    for piece in range(1, GROUP):
        total = total + recv_ref[piece, :PROBES, :].astype(f32)
    return total


def send_all(send_ref, vector, tail):
    for dest in range(GROUP):
        send_ref[dest, :PROBES] = vector
        send_ref[dest, PROBES:] = tail


def after_first(recv_ref, direction_ref, image_ref, send_ref):
    product = total_of(recv_ref)
    direction = direction_ref[...]
    shifted = product + (noise_level - SHIFT_1) * direction
    image_ref[...] = product
    sums = as_rows([lane_sum(direction * shifted), lane_sum(shifted * shifted)])
    send_all(send_ref, shifted.astype(bf16), tail_rows(sums))


def after_second(
    recv_ref, direction_ref, image_ref, pair_ref, known_ref, third_ref, second_ref
):
    along, square = tail_sums((recv_ref,), 2)
    scale = BETA_1 * BETA_1
    alpha_1 = (along + SHIFT_1 * N) / scale
    excess = alpha_1 - SHIFT_1
    squares_2 = jnp.maximum(square - 2.0 * excess * along + excess * excess * N, 0.0) / scale
    beta_2 = jnp.sqrt(squares_2 + epsilon)
    known_ref[...] = stack_rows([alpha_1, beta_2, squares_2], (8, PROBES))
    excess, over, beta = as_columns([excess, 1.0 / beta_2, beta_2 * (1.0 / BETA_1)])
    product = total_of(recv_ref)
    direction, image = direction_ref[...], image_ref[...]
    shifted = image + (noise_level - SHIFT_1) * direction
    second = (shifted - excess * direction) * (1.0 / BETA_1)
    moved = (product - excess * image) * (1.0 / BETA_1)
    third = moved * over - beta * direction
    second_ref[...] = second
    third_ref[...] = third
    for dest in range(GROUP):
        pair_ref[dest, :PROBES] = third.astype(bf16)
        pair_ref[dest, PROBES:] = second.astype(bf16)


def pair_of(right_ref, piece):
    return right_ref[piece, :PROBES, :].astype(f32), right_ref[piece, PROBES:, :].astype(f32)


def join(right_ref, third_ref, send_ref):
    total = jnp.zeros((PROBES, PIECE), f32)
    for piece in range(GROUP):
        third, second = pair_of(right_ref, piece)
        total = total + third * second
    send_all(send_ref, third_ref[...].astype(bf16), tail_rows(as_rows([lane_sum(total)])))


def multiply_third(
    kernel_ref,
    before_ref,
    mine_ref,
    recv_ref,
    first_ref,
    second_ref,
    right_ref,
    known_ref,
    own_third_ref,
    own_second_ref,
    out_ref,
    known_out_ref,
):
    (along,) = tail_sums((mine_ref, recv_ref), 1)
    alpha_1, beta_2, squares_2 = known_ref[0:1], known_ref[1:2], known_ref[2:3]
    scale = beta_2 * beta_2
    curvature = beta_2 * along + scale * alpha_1 * (epsilon / (BETA_1 * BETA_1))
    alpha_2 = (curvature + noise_level * squares_2) / scale
    known_out_ref[...] = stack_rows([alpha_1, beta_2, alpha_2], (8, PROBES))
    turn = (alpha_2 - noise_level) / beta_2
    turn, excess = as_columns([turn, alpha_1 - SHIFT_1])
    slope = turn * (1.0 / BETA_1)
    product = before_ref[...] + multiply(kernel_ref, recv_ref, 1)
    total = jnp.zeros((PROBES, PIECE), f32)
    for piece in range(GROUP):
        cut = span(piece)
        moved = product[:, cut] - slope * (second_ref[:, cut] - excess * first_ref[:, cut])
        third, second = pair_of(right_ref, piece)
        total = total + (third - turn * second) * moved
    own = own_third_ref[...] - turn * own_second_ref[...]
    rows = jnp.concatenate(as_rows([lane_sum(total), lane_sum(own * own)]), axis=1)
    out_ref[...] = jnp.broadcast_to(rows[None], out_ref.shape)


def finish(recv_ref, known_ref, trace_ref, logdet_ref):
    sums = jnp.sum(recv_ref[...], axis=0)
    quad, squares_3 = sums[:, :PROBES], sums[:, PROBES:]
    alpha_1, beta_2, alpha_2 = known_ref[0:1], known_ref[1:2], known_ref[2:3]
    beta_3 = jnp.sqrt(squares_3 + epsilon)
    alpha_3 = (quad + noise_level * squares_3) / (beta_3 * beta_3)
    trace_ref[...] = alpha_1
    logdet_ref[...] = log_weight([alpha_1, alpha_2, alpha_3], [beta_2, beta_3])


def rotation(coupling, difference):
    square = coupling * coupling + difference * difference
    flat = square == 0.0
    inverse = lax.rsqrt(jnp.where(flat, 1.0, square))
    upper = 0.5 + 0.5 * jnp.abs(difference) * inverse
    root = lax.rsqrt(upper)
    large = upper * root
    small = 0.5 * jnp.abs(coupling) * inverse * root
    ahead = difference >= 0.0
    cosine = jnp.where(ahead, large, small)
    sine = jnp.where(ahead, small, large)
    sine = jnp.where(coupling < 0.0, -sine, sine)
    return jnp.where(flat, 1.0, cosine), jnp.where(flat, 0.0, sine)


def log_weight(alpha_list, beta_list):
    zero = jnp.zeros_like(alpha_list[0])
    entry = {(k, k): alpha_list[k] for k in range(3)}
    entry[0, 1], entry[1, 2], entry[0, 2] = beta_list[0], beta_list[1], zero
    first = [zero + 1.0, zero, zero]
    for _ in range(jacobi_sweeps):
        for p, q in ((0, 1), (0, 2), (1, 2)):
            k = 3 - p - q
            pk, qk = (min(p, k), max(p, k)), (min(q, k), max(q, k))
            a, b, d = entry[p, p], entry[p, q], entry[q, q]
            c, s = rotation(2.0 * b, d - a)
            cc, ss, cs = c * c, s * s, c * s
            entry[p, p] = cc * a - 2.0 * cs * b + ss * d
            entry[q, q] = ss * a + 2.0 * cs * b + cc * d
            entry[p, q] = (cc - ss) * b + cs * (a - d)
            entry[pk], entry[qk] = c * entry[pk] - s * entry[qk], s * entry[pk] + c * entry[qk]
            first[p], first[q] = c * first[p] - s * first[q], s * first[p] + c * first[q]
    total = zero
    for k in range(3):
        total = total + first[k] * first[k] * jnp.log(entry[k, k])
    return total


def swap_cores(value):
    return lax.ppermute(value, "core", [(0, 1), (1, 0)])


def exchange(value, axes):
    return lax.all_to_all(value, axes, 0, 0, tiled=True)


def per_device(points, inverse_scales, probe_signs):
    piece = resident((PROBES, PIECE), f32)
    padded = resident((GROUP, PROBES + TAIL, PIECE), bf16)
    block = resident((PROBES, BLOCK), f32)
    send, right, direction = call(
        prepare,
        (
            resident((GROUP, PROBES + 64, PIECE), bf16),
            resident((GROUP, 64, PIECE), bf16),
            piece,
        ),
        points,
        inverse_scales[None],
        probe_signs,
        in_specs=[pl.BlockSpec(memory_space=pl.ANY)] * 3,
        limit=58,
        scratch=[
            pltpu.VMEM((DIM, PIECE), f32),
            pltpu.VMEM((1, DIM), f32),
            pltpu.VMEM((PIECE, PROBES), jnp.int32),
            pltpu.SemaphoreType.DMA((3,)),
        ],
    )
    mine = exchange(send, COL)
    other = swap_cores(mine)
    right = exchange(right, ROW)
    kernel, partial_1, total = call(
        evaluate,
        (
            resident((2 * BLOCK, BLOCK), bf16),
            block,
            resident((GROUP, PROBES, PIECE), bf16),
        ),
        mine,
        other,
        right,
        scratch=[
            pltpu.VMEM((2 * BLOCK, FEATURES), bf16),
            pltpu.VMEM((FEATURES, BLOCK), bf16),
        ],
    )
    recv = exchange(total, ROW)
    image, send = call(after_first, (piece, padded), recv, direction)
    mine = exchange(send, COL)
    other = swap_cores(mine)
    (total,) = call(multiply_first, (block,), kernel, mine)
    partial_2, send = call(multiply_second, (block, padded), kernel, total, mine, other)
    recv = exchange(send, ROW)
    pair, known, third, second = call(
        after_second,
        (
            resident((GROUP, 2 * PROBES, PIECE), bf16),
            resident((8, PROBES), f32),
            piece,
            piece,
        ),
        recv,
        direction,
        image,
    )
    right = exchange(pair, ROW)
    (send,) = call(join, (padded,), right, third)
    mine = exchange(send, COL)
    other = swap_cores(mine)
    (total,) = call(multiply_first, (block,), kernel, mine)
    sums, known = call(
        multiply_third,
        (resident((128, 1, 2 * PROBES), f32), resident((8, PROBES), f32)),
        kernel,
        total,
        mine,
        other,
        partial_1,
        partial_2,
        right,
        known,
        third,
        second,
    )
    row = jax.ShapeDtypeStruct((1, PROBES), f32)
    trace, logdet = call(finish, (row, row), exchange(sums, AXES), known)
    return trace[0], logdet[0]


def solution(mesh):
    split = Mesh(mesh.devices.reshape(2, 4, 2, 4, 2), AXES)
    return jax.shard_map(
        per_device,
        mesh=split,
        in_specs=(P(None, AXES), P(), P(AXES, None)),
        out_specs=(P(), P()),
        check_vma=False,
    )
```

```python
import math

import jax
import jax.numpy as jnp
from jax import lax
from jax.experimental import pallas as pl
from jax.experimental.pallas import tpu as pltpu
from jax.sharding import Mesh
from jax.sharding import PartitionSpec as P

AXES = ("x_lo", "z", "x_hi", "y", "core")
ROW = ("x_lo", "z")
COL = ("x_hi", "y")

N = 32768
DIM = 16
PIECE = 256
PROBES = 128
GROUP = 8
BLOCK = GROUP * PIECE
FEATURES = 128
TAIL = 16

epsilon = 1e-06
noise_level = 1.0
jacobi_sweeps = 6

BETA_1 = math.sqrt(N + epsilon)
SHIFT_1 = 2.0

bf16 = jnp.bfloat16
f32 = jnp.float32


def resident(shape, dtype):
    return pltpu.VMEM(shape, dtype)


def call(body, outs, *args, scratch=(), in_specs=None, limit=12):
    whole = pl.BlockSpec(memory_space=pltpu.VMEM)
    return pl.pallas_call(
        body,
        out_shape=tuple(outs),
        in_specs=in_specs or [whole] * len(args),
        out_specs=tuple([whole] * len(outs)),
        scratch_shapes=list(scratch),
        compiler_params=pltpu.CompilerParams(vmem_limit_bytes=limit * 2**20),
    )(*args)


def parts(value):
    high = value.astype(bf16)
    rest = value - high.astype(f32)
    middle = rest.astype(bf16)
    low = (rest - middle.astype(f32)).astype(bf16)
    return high, middle, low


def stack_rows(values, shape):
    row = lax.broadcasted_iota(jnp.int32, shape, 0)
    block = jnp.zeros(shape, f32)
    for place, value in enumerate(values):
        block = jnp.where(row == place, jnp.broadcast_to(value, shape), block)
    return block


def as_rows(columns):
    lane = lax.broadcasted_iota(jnp.int32, (PROBES, PROBES), 1)
    block = jnp.zeros((PROBES, PROBES), f32)
    for place, value in enumerate(columns):
        block = jnp.where(lane == place, value, block)
    block = block.T
    return [block[place : place + 1] for place in range(len(columns))]


def as_columns(rows):
    block = stack_rows(rows, (PROBES, PROBES)).T
    return [block[:, place : place + 1] for place in range(len(rows))]


def lane_sum(value):
    return jnp.sum(value, axis=1, keepdims=True)


def tail_rows(rows):
    values = [part.astype(f32) for row in rows for part in parts(row)]
    block = stack_rows(values, (TAIL, PROBES))
    return jnp.concatenate([block, jnp.zeros_like(block)], axis=1).astype(bf16)


def total_rows(total, count):
    return [
        total[3 * k : 3 * k + 1] + total[3 * k + 1 : 3 * k + 2] + total[3 * k + 2 : 3 * k + 3]
        for k in range(count)
    ]


def tail_sums(refs, count):
    total = jnp.zeros((TAIL, PROBES), f32)
    for ref in refs:
        for piece in range(GROUP):
            total = total + ref[piece, PROBES:, :PROBES].astype(f32)
    return total_rows(total, count)


def prepare(
    points_hbm,
    scales_hbm,
    signs_hbm,
    send_ref,
    right_ref,
    direction_ref,
    points_ref,
    scales_ref,
    signs_ref,
    sems,
):
    copies = [
        pltpu.make_async_copy(src, dst, sems.at[i])
        for i, (src, dst) in enumerate(
            ((points_hbm, points_ref), (scales_hbm, scales_ref), (signs_hbm, signs_ref))
        )
    ]
    for copy in copies:
        copy.start()
    for copy in copies[:2]:
        copy.wait()
    square = (DIM, DIM)
    same = lax.broadcasted_iota(jnp.int32, square, 0) == lax.broadcasted_iota(jnp.int32, square, 1)
    scales = lane_sum(jnp.where(same, jnp.broadcast_to(scales_ref[...], square), 0.0))
    scaled = points_ref[...] * scales * math.sqrt(math.log2(math.e))
    norms = -0.5 * jnp.sum(scaled * scaled, axis=0, keepdims=True)
    pieces = [part.astype(f32) for part in parts(norms)]
    one = jnp.ones((1, PIECE), f32)
    shape = (16, PIECE)
    points = list(parts(scaled))
    left = jnp.concatenate(points + [stack_rows(pieces + [one] * 3, shape).astype(bf16)], axis=0)
    right = jnp.concatenate(points + [stack_rows([one] * 3 + pieces, shape).astype(bf16)], axis=0)
    for dest in range(GROUP):
        send_ref[dest, PROBES:] = left
        right_ref[dest] = right
    copies[2].wait()
    direction = (2.0 * signs_ref[...].astype(f32) - 1.0).T
    direction_ref[...] = direction
    half = direction.astype(bf16)
    for dest in range(GROUP):
        send_ref[dest, :PROBES] = half


def features(read, order):
    rows = [read(16 * part) for part in order]
    return jnp.concatenate(rows + [jnp.zeros((16, PIECE), bf16)], axis=0)


def wide(ref):
    return jnp.concatenate([ref[piece, :PROBES, :] for piece in range(GROUP)], axis=1)


def span(piece):
    return slice(piece * PIECE, (piece + 1) * PIECE)


def evaluate(mine_ref, other_ref, right_ref, kernel_ref, partial_ref, out_ref, left, right):
    for piece in range(GROUP):
        right[:, span(piece)] = features(
            lambda b: right_ref[piece, b : b + 16, :], (0, 1, 0, 2, 0, 1, 3)
        )
        for half, recv_ref in enumerate((mine_ref, other_ref)):
            left[span(half * GROUP + piece), :] = features(
                lambda b: recv_ref[piece, PROBES + b : PROBES + b + 16, :], (0, 0, 1, 0, 2, 1, 3)
            ).T
    tall = 1024

    def tile(step, carry):
        rows = pl.ds(pl.multiple_of(step * tall, tall), tall)
        for piece in range(GROUP):
            power = jnp.dot(left[rows, :], right[:, span(piece)], preferred_element_type=f32)
            kernel_ref[rows, span(piece)] = jnp.exp2(jnp.minimum(power, 0.0)).astype(bf16)
        return carry

    lax.fori_loop(0, 2 * BLOCK // tall, tile, 0)
    vectors = jnp.concatenate([wide(mine_ref), wide(other_ref)], axis=1)
    total = jnp.dot(vectors, kernel_ref[...], preferred_element_type=f32)
    partial_ref[...] = total
    for piece in range(GROUP):
        out_ref[piece] = total[:, span(piece)].astype(bf16)


def multiply(kernel_ref, recv_ref, half):
    rows = slice(half * BLOCK, (half + 1) * BLOCK)
    return jnp.dot(wide(recv_ref), kernel_ref[rows, :], preferred_element_type=f32)


def multiply_first(kernel_ref, recv_ref, out_ref):
    out_ref[...] = multiply(kernel_ref, recv_ref, 0)


def multiply_second(kernel_ref, before_ref, mine_ref, recv_ref, partial_ref, out_ref):
    total = before_ref[...] + multiply(kernel_ref, recv_ref, 1)
    partial_ref[...] = total
    tail = tail_rows(tail_sums((mine_ref, recv_ref), 2))
    for piece in range(GROUP):
        out_ref[piece, :PROBES] = total[:, span(piece)].astype(bf16)
        out_ref[piece, PROBES:] = tail


def total_of(recv_ref):
    total = recv_ref[0, :PROBES, :].astype(f32)
    for piece in range(1, GROUP):
        total = total + recv_ref[piece, :PROBES, :].astype(f32)
    return total


def send_all(send_ref, vector, tail):
    for dest in range(GROUP):
        send_ref[dest, :PROBES] = vector
        send_ref[dest, PROBES:] = tail


def after_first(recv_ref, direction_ref, image_ref, send_ref):
    product = total_of(recv_ref)
    direction = direction_ref[...]
    shifted = product + (noise_level - SHIFT_1) * direction
    image_ref[...] = product
    sums = as_rows([lane_sum(direction * shifted), lane_sum(shifted * shifted)])
    send_all(send_ref, shifted.astype(bf16), tail_rows(sums))


def after_second(
    recv_ref, direction_ref, image_ref, pair_ref, known_ref, third_ref, second_ref
):
    along, square = tail_sums((recv_ref,), 2)
    scale = BETA_1 * BETA_1
    alpha_1 = (along + SHIFT_1 * N) / scale
    excess = alpha_1 - SHIFT_1
    squares_2 = jnp.maximum(square - 2.0 * excess * along + excess * excess * N, 0.0) / scale
    beta_2 = jnp.sqrt(squares_2 + epsilon)
    known_ref[...] = stack_rows([alpha_1, beta_2, squares_2], (8, PROBES))
    excess, over, beta = as_columns([excess, 1.0 / beta_2, beta_2 * (1.0 / BETA_1)])
    product = total_of(recv_ref)
    direction, image = direction_ref[...], image_ref[...]
    shifted = image + (noise_level - SHIFT_1) * direction
    second = (shifted - excess * direction) * (1.0 / BETA_1)
    moved = (product - excess * image) * (1.0 / BETA_1)
    third = moved * over - beta * direction
    second_ref[...] = second
    third_ref[...] = third
    for dest in range(GROUP):
        pair_ref[dest, :PROBES] = third.astype(bf16)
        pair_ref[dest, PROBES:] = second.astype(bf16)


def pair_of(right_ref, piece):
    return right_ref[piece, :PROBES, :].astype(f32), right_ref[piece, PROBES:, :].astype(f32)


def join(right_ref, third_ref, send_ref):
    total = jnp.zeros((PROBES, PIECE), f32)
    for piece in range(GROUP):
        third, second = pair_of(right_ref, piece)
        total = total + third * second
    send_all(send_ref, third_ref[...].astype(bf16), tail_rows(as_rows([lane_sum(total)])))


def multiply_third(
    kernel_ref,
    before_ref,
    mine_ref,
    recv_ref,
    first_ref,
    second_ref,
    right_ref,
    known_ref,
    own_third_ref,
    own_second_ref,
    out_ref,
    known_out_ref,
):
    (along,) = tail_sums((mine_ref, recv_ref), 1)
    alpha_1, beta_2, squares_2 = known_ref[0:1], known_ref[1:2], known_ref[2:3]
    scale = beta_2 * beta_2
    curvature = beta_2 * along + scale * alpha_1 * (epsilon / (BETA_1 * BETA_1))
    alpha_2 = (curvature + noise_level * squares_2) / scale
    known_out_ref[...] = stack_rows([alpha_1, beta_2, alpha_2], (8, PROBES))
    turn = (alpha_2 - noise_level) / beta_2
    turn, excess = as_columns([turn, alpha_1 - SHIFT_1])
    slope = turn * (1.0 / BETA_1)
    product = before_ref[...] + multiply(kernel_ref, recv_ref, 1)
    total = jnp.zeros((PROBES, PIECE), f32)
    for piece in range(GROUP):
        cut = span(piece)
        moved = product[:, cut] - slope * (second_ref[:, cut] - excess * first_ref[:, cut])
        third, second = pair_of(right_ref, piece)
        total = total + (third - turn * second) * moved
    own = own_third_ref[...] - turn * own_second_ref[...]
    rows = jnp.concatenate(as_rows([lane_sum(total), lane_sum(own * own)]), axis=1)
    out_ref[...] = jnp.broadcast_to(rows[None], out_ref.shape)


def finish(recv_ref, known_ref, trace_ref, logdet_ref):
    sums = jnp.sum(recv_ref[...], axis=0)
    quad, squares_3 = sums[:, :PROBES], sums[:, PROBES:]
    alpha_1, beta_2, alpha_2 = known_ref[0:1], known_ref[1:2], known_ref[2:3]
    beta_3 = jnp.sqrt(squares_3 + epsilon)
    alpha_3 = (quad + noise_level * squares_3) / (beta_3 * beta_3)
    trace_ref[...] = alpha_1
    logdet_ref[...] = log_weight([alpha_1, alpha_2, alpha_3], [beta_2, beta_3])


def rotation(coupling, difference):
    square = coupling * coupling + difference * difference
    flat = square == 0.0
    inverse = lax.rsqrt(jnp.where(flat, 1.0, square))
    upper = 0.5 + 0.5 * jnp.abs(difference) * inverse
    root = lax.rsqrt(upper)
    large = upper * root
    small = 0.5 * jnp.abs(coupling) * inverse * root
    ahead = difference >= 0.0
    cosine = jnp.where(ahead, large, small)
    sine = jnp.where(ahead, small, large)
    sine = jnp.where(coupling < 0.0, -sine, sine)
    return jnp.where(flat, 1.0, cosine), jnp.where(flat, 0.0, sine)


def log_weight(alpha_list, beta_list):
    zero = jnp.zeros_like(alpha_list[0])
    entry = {(k, k): alpha_list[k] for k in range(3)}
    entry[0, 1], entry[1, 2], entry[0, 2] = beta_list[0], beta_list[1], zero
    first = [zero + 1.0, zero, zero]
    for _ in range(jacobi_sweeps):
        for p, q in ((0, 1), (0, 2), (1, 2)):
            k = 3 - p - q
            pk, qk = (min(p, k), max(p, k)), (min(q, k), max(q, k))
            a, b, d = entry[p, p], entry[p, q], entry[q, q]
            c, s = rotation(2.0 * b, d - a)
            cc, ss, cs = c * c, s * s, c * s
            entry[p, p] = cc * a - 2.0 * cs * b + ss * d
            entry[q, q] = ss * a + 2.0 * cs * b + cc * d
            entry[p, q] = (cc - ss) * b + cs * (a - d)
            entry[pk], entry[qk] = c * entry[pk] - s * entry[qk], s * entry[pk] + c * entry[qk]
            first[p], first[q] = c * first[p] - s * first[q], s * first[p] + c * first[q]
    total = zero
    for k in range(3):
        total = total + first[k] * first[k] * jnp.log(entry[k, k])
    return total


def swap_cores(value):
    return lax.ppermute(value, "core", [(0, 1), (1, 0)])


def exchange(value, axes):
    return lax.all_to_all(value, axes, 0, 0, tiled=True)


def per_device(points, inverse_scales, probe_signs):
    piece = resident((PROBES, PIECE), f32)
    padded = resident((GROUP, PROBES + TAIL, PIECE), bf16)
    block = resident((PROBES, BLOCK), f32)
    send, right, direction = call(
        prepare,
        (
            resident((GROUP, PROBES + 64, PIECE), bf16),
            resident((GROUP, 64, PIECE), bf16),
            piece,
        ),
        points,
        inverse_scales[None],
        probe_signs,
        in_specs=[pl.BlockSpec(memory_space=pl.ANY)] * 3,
        limit=58,
        scratch=[
            pltpu.VMEM((DIM, PIECE), f32),
            pltpu.VMEM((1, DIM), f32),
            pltpu.VMEM((PIECE, PROBES), jnp.int32),
            pltpu.SemaphoreType.DMA((3,)),
        ],
    )
    mine = exchange(send, COL)
    other = swap_cores(mine)
    right = exchange(right, ROW)
    kernel, partial_1, total = call(
        evaluate,
        (
            resident((2 * BLOCK, BLOCK), bf16),
            block,
            resident((GROUP, PROBES, PIECE), bf16),
        ),
        mine,
        other,
        right,
        scratch=[
            pltpu.VMEM((2 * BLOCK, FEATURES), bf16),
            pltpu.VMEM((FEATURES, BLOCK), bf16),
        ],
    )
    recv = exchange(total, ROW)
    image, send = call(after_first, (piece, padded), recv, direction)
    mine = exchange(send, COL)
    other = swap_cores(mine)
    (total,) = call(multiply_first, (block,), kernel, mine)
    partial_2, send = call(multiply_second, (block, padded), kernel, total, mine, other)
    recv = exchange(send, ROW)
    pair, known, third, second = call(
        after_second,
        (
            resident((GROUP, 2 * PROBES, PIECE), bf16),
            resident((8, PROBES), f32),
            piece,
            piece,
        ),
        recv,
        direction,
        image,
    )
    right = exchange(pair, ROW)
    (send,) = call(join, (padded,), right, third)
    mine = exchange(send, COL)
    other = swap_cores(mine)
    (total,) = call(multiply_first, (block,), kernel, mine)
    sums, known = call(
        multiply_third,
        (resident((128, 1, 2 * PROBES), f32), resident((8, PROBES), f32)),
        kernel,
        total,
        mine,
        other,
        partial_1,
        partial_2,
        right,
        known,
        third,
        second,
    )
    row = jax.ShapeDtypeStruct((1, PROBES), f32)
    trace, logdet = call(finish, (row, row), exchange(sums, AXES), known)
    return trace[0], logdet[0]


def solution(mesh):
    split = Mesh(mesh.devices.reshape(2, 4, 2, 4, 2), AXES)
    return jax.shard_map(
        per_device,
        mesh=split,
        in_specs=(P(None, AXES), P(), P(AXES, None)),
        out_specs=(P(), P()),
        check_vma=False,
    )
```

```python
import math

import jax
import jax.numpy as jnp
from jax import lax
from jax.experimental import pallas as pl
from jax.experimental.pallas import tpu as pltpu
from jax.sharding import Mesh
from jax.sharding import PartitionSpec as P

AXES = ("x_lo", "z", "x_hi", "y", "core")
ROW = ("z", "x_lo")
COL = ("y", "x_hi")

N = 32768
DIM = 16
PIECE = 256
PROBES = 128
GROUP = 8
BLOCK = GROUP * PIECE
FEATURES = 128
TAIL = 16

epsilon = 1e-06
noise_level = 1.0
jacobi_sweeps = 6

BETA_1 = math.sqrt(N + epsilon)
SHIFT_1 = 2.0

bf16 = jnp.bfloat16
f32 = jnp.float32


def resident(shape, dtype):
    return pltpu.VMEM(shape, dtype)


def call(body, outs, *args, scratch=(), in_specs=None, limit=12):
    whole = pl.BlockSpec(memory_space=pltpu.VMEM)
    return pl.pallas_call(
        body,
        out_shape=tuple(outs),
        in_specs=in_specs or [whole] * len(args),
        out_specs=tuple([whole] * len(outs)),
        scratch_shapes=list(scratch),
        compiler_params=pltpu.CompilerParams(vmem_limit_bytes=limit * 2**20),
    )(*args)


def parts(value):
    high = value.astype(bf16)
    rest = value - high.astype(f32)
    middle = rest.astype(bf16)
    low = (rest - middle.astype(f32)).astype(bf16)
    return high, middle, low


def stack_rows(values, shape):
    row = lax.broadcasted_iota(jnp.int32, shape, 0)
    block = jnp.zeros(shape, f32)
    for place, value in enumerate(values):
        block = jnp.where(row == place, jnp.broadcast_to(value, shape), block)
    return block


def as_rows(columns):
    lane = lax.broadcasted_iota(jnp.int32, (PROBES, PROBES), 1)
    block = jnp.zeros((PROBES, PROBES), f32)
    for place, value in enumerate(columns):
        block = jnp.where(lane == place, value, block)
    block = block.T
    return [block[place : place + 1] for place in range(len(columns))]


def as_columns(rows):
    block = stack_rows(rows, (PROBES, PROBES)).T
    return [block[:, place : place + 1] for place in range(len(rows))]


def lane_sum(value):
    return jnp.sum(value, axis=1, keepdims=True)


def tail_rows(rows):
    values = [part.astype(f32) for row in rows for part in parts(row)]
    block = stack_rows(values, (TAIL, PROBES))
    return jnp.concatenate([block, jnp.zeros_like(block)], axis=1).astype(bf16)


def total_rows(total, count):
    return [
        total[3 * k : 3 * k + 1] + total[3 * k + 1 : 3 * k + 2] + total[3 * k + 2 : 3 * k + 3]
        for k in range(count)
    ]


def tail_sums(refs, count):
    total = jnp.zeros((TAIL, PROBES), f32)
    for ref in refs:
        for piece in range(GROUP):
            total = total + ref[piece, PROBES:, :PROBES].astype(f32)
    return total_rows(total, count)


def prepare(
    points_hbm,
    scales_hbm,
    signs_hbm,
    send_ref,
    right_ref,
    direction_ref,
    points_ref,
    scales_ref,
    signs_ref,
    sems,
):
    copies = [
        pltpu.make_async_copy(src, dst, sems.at[i])
        for i, (src, dst) in enumerate(
            ((points_hbm, points_ref), (scales_hbm, scales_ref), (signs_hbm, signs_ref))
        )
    ]
    for copy in copies:
        copy.start()
    for copy in copies[:2]:
        copy.wait()
    square = (DIM, DIM)
    same = lax.broadcasted_iota(jnp.int32, square, 0) == lax.broadcasted_iota(jnp.int32, square, 1)
    scales = lane_sum(jnp.where(same, jnp.broadcast_to(scales_ref[...], square), 0.0))
    scaled = points_ref[...] * scales * math.sqrt(math.log2(math.e))
    norms = -0.5 * jnp.sum(scaled * scaled, axis=0, keepdims=True)
    pieces = [part.astype(f32) for part in parts(norms)]
    one = jnp.ones((1, PIECE), f32)
    shape = (16, PIECE)
    points = list(parts(scaled))
    left = jnp.concatenate(points + [stack_rows(pieces + [one] * 3, shape).astype(bf16)], axis=0)
    right = jnp.concatenate(points + [stack_rows([one] * 3 + pieces, shape).astype(bf16)], axis=0)
    for dest in range(GROUP):
        send_ref[dest, PROBES:] = left
        right_ref[dest] = right
    copies[2].wait()
    direction = (2.0 * signs_ref[...].astype(f32) - 1.0).T
    direction_ref[...] = direction
    half = direction.astype(bf16)
    for dest in range(GROUP):
        send_ref[dest, :PROBES] = half


def features(read, order):
    rows = [read(16 * part) for part in order]
    return jnp.concatenate(rows + [jnp.zeros((16, PIECE), bf16)], axis=0)


def wide(ref):
    return jnp.concatenate([ref[piece, :PROBES, :] for piece in range(GROUP)], axis=1)


def span(piece):
    return slice(piece * PIECE, (piece + 1) * PIECE)


def evaluate(mine_ref, other_ref, right_ref, kernel_ref, partial_ref, out_ref, left, right):
    for piece in range(GROUP):
        right[:, span(piece)] = features(
            lambda b: right_ref[piece, b : b + 16, :], (0, 1, 0, 2, 0, 1, 3)
        )
        for half, recv_ref in enumerate((mine_ref, other_ref)):
            left[span(half * GROUP + piece), :] = features(
                lambda b: recv_ref[piece, PROBES + b : PROBES + b + 16, :], (0, 0, 1, 0, 2, 1, 3)
            ).T
    tall = 1024

    def tile(step, carry):
        rows = pl.ds(pl.multiple_of(step * tall, tall), tall)
        for piece in range(GROUP):
            power = jnp.dot(left[rows, :], right[:, span(piece)], preferred_element_type=f32)
            kernel_ref[rows, span(piece)] = jnp.exp2(jnp.minimum(power, 0.0)).astype(bf16)
        return carry

    lax.fori_loop(0, 2 * BLOCK // tall, tile, 0)
    vectors = jnp.concatenate([wide(mine_ref), wide(other_ref)], axis=1)
    total = jnp.dot(vectors, kernel_ref[...], preferred_element_type=f32)
    partial_ref[...] = total
    for piece in range(GROUP):
        out_ref[piece] = total[:, span(piece)].astype(bf16)


def multiply(kernel_ref, recv_ref, half):
    rows = slice(half * BLOCK, (half + 1) * BLOCK)
    return jnp.dot(wide(recv_ref), kernel_ref[rows, :], preferred_element_type=f32)


def multiply_first(kernel_ref, recv_ref, out_ref):
    out_ref[...] = multiply(kernel_ref, recv_ref, 0)


def multiply_second(kernel_ref, before_ref, mine_ref, recv_ref, partial_ref, out_ref):
    total = before_ref[...] + multiply(kernel_ref, recv_ref, 1)
    partial_ref[...] = total
    tail = tail_rows(tail_sums((mine_ref, recv_ref), 2))
    for piece in range(GROUP):
        out_ref[piece, :PROBES] = total[:, span(piece)].astype(bf16)
        out_ref[piece, PROBES:] = tail


def total_of(recv_ref):
    total = recv_ref[0, :PROBES, :].astype(f32)
    for piece in range(1, GROUP):
        total = total + recv_ref[piece, :PROBES, :].astype(f32)
    return total


def send_all(send_ref, vector, tail):
    for dest in range(GROUP):
        send_ref[dest, :PROBES] = vector
        send_ref[dest, PROBES:] = tail


def after_first(recv_ref, direction_ref, image_ref, send_ref):
    product = total_of(recv_ref)
    direction = direction_ref[...]
    shifted = product + (noise_level - SHIFT_1) * direction
    image_ref[...] = product
    sums = as_rows([lane_sum(direction * shifted), lane_sum(shifted * shifted)])
    send_all(send_ref, shifted.astype(bf16), tail_rows(sums))


def after_second(
    recv_ref, direction_ref, image_ref, pair_ref, known_ref, third_ref, second_ref
):
    along, square = tail_sums((recv_ref,), 2)
    scale = BETA_1 * BETA_1
    alpha_1 = (along + SHIFT_1 * N) / scale
    excess = alpha_1 - SHIFT_1
    squares_2 = jnp.maximum(square - 2.0 * excess * along + excess * excess * N, 0.0) / scale
    beta_2 = jnp.sqrt(squares_2 + epsilon)
    known_ref[...] = stack_rows([alpha_1, beta_2, squares_2], (8, PROBES))
    excess, over, beta = as_columns([excess, 1.0 / beta_2, beta_2 * (1.0 / BETA_1)])
    product = total_of(recv_ref)
    direction, image = direction_ref[...], image_ref[...]
    shifted = image + (noise_level - SHIFT_1) * direction
    second = (shifted - excess * direction) * (1.0 / BETA_1)
    moved = (product - excess * image) * (1.0 / BETA_1)
    third = moved * over - beta * direction
    second_ref[...] = second
    third_ref[...] = third
    for dest in range(GROUP):
        pair_ref[dest, :PROBES] = third.astype(bf16)
        pair_ref[dest, PROBES:] = second.astype(bf16)


def pair_of(right_ref, piece):
    return right_ref[piece, :PROBES, :].astype(f32), right_ref[piece, PROBES:, :].astype(f32)


def join(right_ref, third_ref, send_ref):
    total = jnp.zeros((PROBES, PIECE), f32)
    for piece in range(GROUP):
        third, second = pair_of(right_ref, piece)
        total = total + third * second
    send_all(send_ref, third_ref[...].astype(bf16), tail_rows(as_rows([lane_sum(total)])))


def multiply_third(
    kernel_ref,
    before_ref,
    mine_ref,
    recv_ref,
    first_ref,
    second_ref,
    right_ref,
    known_ref,
    own_third_ref,
    own_second_ref,
    out_ref,
    known_out_ref,
):
    (along,) = tail_sums((mine_ref, recv_ref), 1)
    alpha_1, beta_2, squares_2 = known_ref[0:1], known_ref[1:2], known_ref[2:3]
    scale = beta_2 * beta_2
    curvature = beta_2 * along + scale * alpha_1 * (epsilon / (BETA_1 * BETA_1))
    alpha_2 = (curvature + noise_level * squares_2) / scale
    known_out_ref[...] = stack_rows([alpha_1, beta_2, alpha_2], (8, PROBES))
    turn = (alpha_2 - noise_level) / beta_2
    turn, excess = as_columns([turn, alpha_1 - SHIFT_1])
    slope = turn * (1.0 / BETA_1)
    product = before_ref[...] + multiply(kernel_ref, recv_ref, 1)
    total = jnp.zeros((PROBES, PIECE), f32)
    for piece in range(GROUP):
        cut = span(piece)
        moved = product[:, cut] - slope * (second_ref[:, cut] - excess * first_ref[:, cut])
        third, second = pair_of(right_ref, piece)
        total = total + (third - turn * second) * moved
    own = own_third_ref[...] - turn * own_second_ref[...]
    rows = jnp.concatenate(as_rows([lane_sum(total), lane_sum(own * own)]), axis=1)
    out_ref[...] = jnp.broadcast_to(rows[None], out_ref.shape)


def finish(recv_ref, known_ref, trace_ref, logdet_ref):
    sums = jnp.sum(recv_ref[...], axis=0)
    quad, squares_3 = sums[:, :PROBES], sums[:, PROBES:]
    alpha_1, beta_2, alpha_2 = known_ref[0:1], known_ref[1:2], known_ref[2:3]
    beta_3 = jnp.sqrt(squares_3 + epsilon)
    alpha_3 = (quad + noise_level * squares_3) / (beta_3 * beta_3)
    trace_ref[...] = alpha_1
    logdet_ref[...] = log_weight([alpha_1, alpha_2, alpha_3], [beta_2, beta_3])


def rotation(coupling, difference):
    square = coupling * coupling + difference * difference
    flat = square == 0.0
    inverse = lax.rsqrt(jnp.where(flat, 1.0, square))
    upper = 0.5 + 0.5 * jnp.abs(difference) * inverse
    root = lax.rsqrt(upper)
    large = upper * root
    small = 0.5 * jnp.abs(coupling) * inverse * root
    ahead = difference >= 0.0
    cosine = jnp.where(ahead, large, small)
    sine = jnp.where(ahead, small, large)
    sine = jnp.where(coupling < 0.0, -sine, sine)
    return jnp.where(flat, 1.0, cosine), jnp.where(flat, 0.0, sine)


def log_weight(alpha_list, beta_list):
    zero = jnp.zeros_like(alpha_list[0])
    entry = {(k, k): alpha_list[k] for k in range(3)}
    entry[0, 1], entry[1, 2], entry[0, 2] = beta_list[0], beta_list[1], zero
    first = [zero + 1.0, zero, zero]
    for _ in range(jacobi_sweeps):
        for p, q in ((0, 1), (0, 2), (1, 2)):
            k = 3 - p - q
            pk, qk = (min(p, k), max(p, k)), (min(q, k), max(q, k))
            a, b, d = entry[p, p], entry[p, q], entry[q, q]
            c, s = rotation(2.0 * b, d - a)
            cc, ss, cs = c * c, s * s, c * s
            entry[p, p] = cc * a - 2.0 * cs * b + ss * d
            entry[q, q] = ss * a + 2.0 * cs * b + cc * d
            entry[p, q] = (cc - ss) * b + cs * (a - d)
            entry[pk], entry[qk] = c * entry[pk] - s * entry[qk], s * entry[pk] + c * entry[qk]
            first[p], first[q] = c * first[p] - s * first[q], s * first[p] + c * first[q]
    total = zero
    for k in range(3):
        total = total + first[k] * first[k] * jnp.log(entry[k, k])
    return total


def swap_cores(value):
    return lax.ppermute(value, "core", [(0, 1), (1, 0)])


def exchange(value, axes):
    return lax.all_to_all(value, axes, 0, 0, tiled=True)


def per_device(points, inverse_scales, probe_signs):
    piece = resident((PROBES, PIECE), f32)
    padded = resident((GROUP, PROBES + TAIL, PIECE), bf16)
    block = resident((PROBES, BLOCK), f32)
    send, right, direction = call(
        prepare,
        (
            resident((GROUP, PROBES + 64, PIECE), bf16),
            resident((GROUP, 64, PIECE), bf16),
            piece,
        ),
        points,
        inverse_scales[None],
        probe_signs,
        in_specs=[pl.BlockSpec(memory_space=pl.ANY)] * 3,
        limit=58,
        scratch=[
            pltpu.VMEM((DIM, PIECE), f32),
            pltpu.VMEM((1, DIM), f32),
            pltpu.VMEM((PIECE, PROBES), jnp.int32),
            pltpu.SemaphoreType.DMA((3,)),
        ],
    )
    mine = exchange(send, COL)
    other = swap_cores(mine)
    right = exchange(right, ROW)
    kernel, partial_1, total = call(
        evaluate,
        (
            resident((2 * BLOCK, BLOCK), bf16),
            block,
            resident((GROUP, PROBES, PIECE), bf16),
        ),
        mine,
        other,
        right,
        scratch=[
            pltpu.VMEM((2 * BLOCK, FEATURES), bf16),
            pltpu.VMEM((FEATURES, BLOCK), bf16),
        ],
    )
    recv = exchange(total, ROW)
    image, send = call(after_first, (piece, padded), recv, direction)
    mine = exchange(send, COL)
    other = swap_cores(mine)
    (total,) = call(multiply_first, (block,), kernel, mine)
    partial_2, send = call(multiply_second, (block, padded), kernel, total, mine, other)
    recv = exchange(send, ROW)
    pair, known, third, second = call(
        after_second,
        (
            resident((GROUP, 2 * PROBES, PIECE), bf16),
            resident((8, PROBES), f32),
            piece,
            piece,
        ),
        recv,
        direction,
        image,
    )
    right = exchange(pair, ROW)
    (send,) = call(join, (padded,), right, third)
    mine = exchange(send, COL)
    other = swap_cores(mine)
    (total,) = call(multiply_first, (block,), kernel, mine)
    sums, known = call(
        multiply_third,
        (resident((128, 1, 2 * PROBES), f32), resident((8, PROBES), f32)),
        kernel,
        total,
        mine,
        other,
        partial_1,
        partial_2,
        right,
        known,
        third,
        second,
    )
    row = jax.ShapeDtypeStruct((1, PROBES), f32)
    trace, logdet = call(finish, (row, row), exchange(sums, AXES), known)
    return trace[0], logdet[0]


def solution(mesh):
    split = Mesh(mesh.devices.reshape(2, 4, 2, 4, 2), AXES)
    return jax.shard_map(
        per_device,
        mesh=split,
        in_specs=(P(None, AXES), P(), P(AXES, None)),
        out_specs=(P(), P()),
        check_vma=False,
    )
```
